256 devices in a mesh: wide: 64 (over y_hi, z, x), narrow: 4 (over y_lo, core).
Axes of the slice: x: 4, y: 4 (y_hi: 2, y_lo: 2; y = y_hi * 2 + y_lo), z: 8, core: 2. Of those that a mesh axis runs over, the one named last changes fastest.
Arguments:
- volume: bfloat16 [128, 16, 64, 256], P('wide', 'narrow'), may hold values from -6 to 6
- volume_tangent: bfloat16 [128, 16, 64, 256], P('wide', 'narrow'), may hold values from -6 to 6
- shallow_weight: bfloat16 [3, 3, 3, 64, 64], replicated, may hold values from -0.15625 to 0.15625
- deep_weight: bfloat16 [3, 3, 3, 64, 256], replicated, may hold values from -0.15625 to 0.15625
Outputs:
- skip_features: bfloat16 [128, 16, 64, 256], P('wide', 'narrow')
- skip_tangent: bfloat16 [128, 16, 64, 256], P('wide', 'narrow')
- deep_features: bfloat16 [64, 8, 256, 128], P('wide', None, 'narrow')
- deep_tangent: bfloat16 [64, 8, 256, 128], P('wide', None, 'narrow')
The draws below stay inside these ranges and needn't reach their ends.
All inputs are finite; a program needn't handle non-finite values.
Results may differ from the reference program's by a relative error of at most 0.0058.
Values may be sent and summed in bfloat16 or wider, within the bound.
No kernel may reach another device: no remote copies, remote signals or barrier semaphores. Data moves between devices by JAX's collectives and lax.ppermute only.
A program may use at most 64 MiB of HBM per device.

```python
import math
import jax
import jax.numpy as jnp
from jax import lax

C1 = 64
C2 = 256
XS = 256
NZ = 128
NY = 16


def block_scale(own_key, shape, shards, smallest, top_value):
    gain = 1.0
    for dim, blocks in shards:
        draws = jax.random.uniform(jax.random.fold_in(jax.random.fold_in(own_key, 6), dim), (blocks,), jnp.float32, smallest / len(shards), top_value / len(shards))
        gain = gain * jnp.repeat(jnp.exp(draws), shape[dim] // blocks).reshape((-1,) + (1,) * (len(shape) - 1 - dim))
    return gain


def normal_values(rng, extent, deviation, reach, shards=(), kind=jnp.bfloat16):
    values = jax.random.normal(rng, extent, jnp.float32) * deviation
    if len(shards) > 0:
        values = block_scale(rng, extent, shards, -0.22, 0.18) * values
    return jnp.clip(values, min=-reach, max=reach).astype(kind)


def setup_inputs(seed: int = 0) -> dict:
    streams_of = jax.random.split(jax.random.key(seed), 5)
    return {
        "volume": normal_values(streams_of[0], (NZ, NY, C1, XS), 1.0, 6.0, ((0, 64), (1, 4))),
        "volume_tangent": normal_values(streams_of[1], (NZ, NY, C1, XS), 1.0, 6.0, ((0, 64), (1, 4))),
        "shallow_weight": normal_values(streams_of[2], (3, 3, 3, C1, C1), (27 * C1) ** -0.5, 0.15625),
        "deep_weight": normal_values(streams_of[3], (3, 3, 3, C1, C2), (27 * C1) ** -0.5, 0.15625),
    }


def conv_taps(padded, weight):
    count = padded.shape[0]
    planes = padded.shape[1] - 2
    rows_y = padded.shape[2] - 2
    cells_x = padded.shape[4]
    channels = weight.shape[3]
    outputs = weight.shape[4]
    extended = jnp.pad(padded, ((0, 0), (0, 0), (0, 0), (0, 0), (1, 1)))
    summed = None
    for step_z in range(3):
        for step_y in range(3):
            layer = extended[:, step_z:step_z + planes, step_y:step_y + rows_y]
            stacked = jnp.concatenate([layer[..., step_x:step_x + cells_x] for step_x in range(3)], axis=3)
            kernel = weight[step_z, step_y].reshape(3 * channels, outputs)
            flat = jnp.transpose(stacked, (3, 0, 1, 2, 4)).reshape(3 * channels, -1)
            product = jnp.dot(kernel.T, flat, preferred_element_type=jnp.float32)
            product = product.reshape(outputs, count, planes, rows_y, cells_x)
            partial_sum = jnp.transpose(product, (1, 2, 3, 0, 4))
            summed = partial_sum if summed is None else summed + partial_sum
    return summed


def activate(preact):
    sigmoid_v = jax.nn.sigmoid(preact[0])
    primal = (preact[0] * sigmoid_v).astype(jnp.bfloat16)
    slope = sigmoid_v * (1.0 + preact[0] * (1.0 - sigmoid_v))
    tangent = (slope * preact[1]).astype(jnp.bfloat16)
    return primal, tangent


def average_pool(stacked):
    count, planes, rows_y, channels, cells_x = stacked.shape
    blocks = stacked.astype(jnp.float32).reshape(count, planes // 2, 2, rows_y // 2, 2, channels, cells_x // 2, 2)
    return jnp.mean(blocks, axis=(2, 4, 7)).astype(jnp.bfloat16)


def convolve_act(stacked, weight):
    planes = stacked.shape[1]
    block_size = math.gcd(planes, 8)
    padded = jnp.pad(stacked, ((0, 0), (1, 1), (1, 1), (0, 0), (0, 0)))

    def one_block(offset):
        window = lax.dynamic_slice_in_dim(padded, offset, block_size + 2, 1)
        return activate(conv_taps(window, weight))

    offsets = jnp.arange(planes // block_size, dtype=jnp.int32) * block_size
    primal, tangent = lax.map(one_block, offsets)
    primal = primal.reshape((planes,) + primal.shape[2:])
    tangent = tangent.reshape((planes,) + tangent.shape[2:])
    return primal, tangent


def reference(volume, volume_tangent, shallow_weight, deep_weight):
    skip_features, skip_tangent = convolve_act(jnp.stack([volume, volume_tangent]), shallow_weight)
    pooled = average_pool(jnp.stack([skip_features, skip_tangent]))
    deep_features, deep_tangent = convolve_act(pooled, deep_weight)
    return skip_features, skip_tangent, deep_features, deep_tangent
```

```python
import functools

import jax
import jax.numpy as jnp
from jax import lax
from jax.experimental import pallas as pl
from jax.experimental.pallas import tpu as pltpu
from jax.sharding import PartitionSpec as P

BOTH = ("wide", "narrow")
BF16 = jnp.bfloat16
F32 = jnp.float32
ANY = pl.BlockSpec(memory_space=pl.ANY)
VMEM = pl.BlockSpec(memory_space=pltpu.VMEM)


def exchange(wide, narrow, kind, route):
    pairs = []
    for w in range(wide):
        for n in range(narrow):
            if kind == "E":
                pw = w ^ 1
            elif kind == "O":
                pw = w + 1 if w % 2 else w - 1
            else:
                pw = w
            if not 0 <= pw < wide:
                pw, pn = w, n ^ 1
            elif route == "same" or (route == "near" and min(w, pw) != wide // 2 - 1):
                pn = n
            elif route == "core":
                pn = n ^ 1
            elif route == "mirror":
                pn = narrow - 1 - n
            else:
                pn = n ^ 2
            pairs.append((w * narrow + n, pw * narrow + pn))
    return pairs


def start_copies(copies, sems):
    for k, (cond, src, dst) in enumerate(copies):
        copy = pltpu.make_async_copy(src, dst, sems.at[k])
        if cond is None:
            copy.start()
        else:
            pl.when(cond)(copy.start)


def wait_copies(copies, sems):
    for k, (cond, src, dst) in enumerate(copies):
        copy = pltpu.make_async_copy(src, dst, sems.at[k])
        if cond is None:
            copy.wait()
        else:
            pl.when(cond)(copy.wait)


def slices_kernel(vol, tan, s_o, s_e, s_c, s_m, s_do, s_de, sems):
    w, n = lax.axis_index("wide"), lax.axis_index("narrow")
    last = vol.shape[1] - 1
    odd = lax.rem(w, 2)
    row_c = jnp.where(lax.rem(n, 2) == 0, last, 0)
    row_m = jnp.where(n < 2, last, 0)
    copies = []
    for t, src in enumerate((vol, tan)):
        copies.append((None, src.at[odd], s_o.at[t]))
    for t, src in enumerate((vol, tan)):
        copies.append((None, src.at[odd, row_m], s_do.at[t]))
        copies.append((None, src.at[1 - odd], s_e.at[t]))
        copies.append((None, src.at[1 - odd, row_m], s_de.at[t]))
        copies.append((None, src.at[:, row_c], s_c.at[t]))
        copies.append((None, src.at[:, row_m], s_m.at[t]))
    start_copies(copies, sems)
    wait_copies(copies, sems)


def weights_kernel(sw, dw, t_s, t_d, dw_half, band, dband, sem):
    n = lax.axis_index("narrow")
    copy = pltpu.make_async_copy(
        dw.at[:, :, :, :, pl.ds(pl.multiple_of((n // 2) * 128, 128), 128)], dw_half, sem
    )
    copy.start()
    band[...] = jnp.zeros_like(band)
    dband[...] = jnp.zeros_like(dband)
    nt = (((1,), (1,)), ((), ()))

    def build(source, scratch, pick, out):
        for a in range(3):
            for c in range(3):
                for b in range(3):
                    scratch[a * 3 + c, 64 * (b + 1) : 64 * (b + 2), :] = source[a, b, c]
                for r in range(2):
                    rows = scratch[a * 3 + c, 64 * (1 - r) : 64 * (1 - r) + 256, :]
                    placed = lax.dot_general(pick, rows, nt, preferred_element_type=F32)
                    out[c * 128 + r * 64 : c * 128 + r * 64 + 64, a * 256 : a * 256 + 256] = (
                        placed.astype(BF16)
                    )

    def selector(width, shift):
        row = lax.broadcasted_iota(jnp.int32, (64, width), 0)
        col = lax.broadcasted_iota(jnp.int32, (64, width), 1)
        return jnp.where(col == row + shift, 1.0, 0.0).astype(BF16)

    build(sw, band, selector(64, 0), t_s)
    copy.wait()
    build(dw_half, dband, selector(128, 64 * lax.rem(n, 2)), t_d)


def shifted_sum(acc, lane, first, final):
    left = pltpu.roll(acc[0:128], 1, 1)
    right = pltpu.roll(acc[256:384], acc.shape[1] - 1, 1)
    return acc[128:256] + jnp.where(first(lane), 0.0, left) + jnp.where(final(lane), 0.0, right)


def activate(pre, dot):
    s = 0.5 * jnp.tanh(0.5 * pre) + 0.5
    primal = (pre * s).astype(BF16)
    tangent = (s * (1.0 + pre * (1.0 - s)) * dot).astype(BF16)
    return primal, tangent


def shallow_kernel(wide, narrow, vol, tan, r_o, r_e, r_c, r_m, c_o, c_e, d_o, d_e, t_s,
                   skip_f, skip_t, pooled, x, sems):
    w, n = lax.axis_index("wide"), lax.axis_index("narrow")
    odd = lax.rem(w, 2)
    rows = vol.shape[1]
    plane_o, plane_e = 3 * odd, 3 * (1 - odd)
    slot_c = jnp.where(lax.rem(n, 2) == 0, rows + 1, 0)
    slot_m = jnp.where(lax.rem(n, 2) == 0, 0, rows + 1)
    has_o = (w > 0) & (w < wide - 1)
    has_m = (n > 0) & (n < narrow - 1)
    both = has_o & has_m
    copies = []
    for t, src in enumerate((vol, tan)):
        copies += [
            (None, src, x.at[t, pl.ds(1, 2), pl.ds(1, rows)]),
            (None, r_c.at[t], x.at[t, pl.ds(1, 2), slot_c]),
            (has_m, r_m.at[t], x.at[t, pl.ds(1, 2), slot_m]),
            (None, r_e.at[t], x.at[t, plane_e, pl.ds(1, rows)]),
            (None, c_e.at[t], x.at[t, plane_e, slot_c]),
            (has_m, d_e.at[t], x.at[t, plane_e, slot_m]),
            (has_o, r_o.at[t], x.at[t, plane_o, pl.ds(1, rows)]),
            (has_o, c_o.at[t], x.at[t, plane_o, slot_c]),
            (both, d_o.at[t], x.at[t, plane_o, slot_m]),
        ]
    start_copies(copies, sems)

    @pl.when(jnp.logical_not(has_o))
    def _():
        for t in range(2):
            x[t, plane_o] = jnp.zeros(x.shape[2:], BF16)

    @pl.when(jnp.logical_not(has_m))
    def _():
        for t in range(2):
            for p in range(4):
                x[t, p, slot_m] = jnp.zeros(x.shape[3:], BF16)

    cells = vol.shape[3]
    lane = lax.broadcasted_iota(jnp.int32, (128, cells), 1)
    first, final = (lambda v: v == 0), (lambda v: v == cells - 1)
    source = lax.broadcasted_iota(jnp.int32, (cells, cells // 2), 0)
    target = lax.broadcasted_iota(jnp.int32, (cells, cells // 2), 1)
    pairing = jnp.where(source // 2 == target, 0.125, 0.0).astype(BF16)
    wait_copies(copies, sems)
    for win in range(rows // 2):
        sums = [None, None]
        for q in range(2):
            pre = []
            for t in range(2):
                stack = jnp.concatenate(
                    [x[t, q + a, 2 * win : 2 * win + 4].reshape(256, cells) for a in range(3)], axis=0
                )
                acc = jnp.dot(t_s[...], stack, preferred_element_type=F32)
                pre.append(shifted_sum(acc, lane, first, final))
            out = activate(*pre)
            for t, ref in enumerate((skip_f, skip_t)):
                ref[q, 2 * win : 2 * win + 2] = out[t].reshape(2, 64, cells)
                half = jnp.dot(out[t], pairing, preferred_element_type=F32)
                half = half[0:64] + half[64:128]
                sums[t] = half if sums[t] is None else sums[t] + half
        pooled[win] = jnp.concatenate(sums, axis=1).astype(BF16)


def deep_kernel(wide, narrow, own, other, g_c, r_o, r_e, o_c, e_c, t_d, out_f, out_t, x, sems):
    w, n = lax.axis_index("wide"), lax.axis_index("narrow")
    odd = lax.rem(w, 2)
    plane_o, plane_e = 2 * odd, 2 * (1 - odd)
    has_o = (w > 0) & (w < wide - 1)
    far = (w == wide // 2 - 1) | (w == wide // 2)
    core = lax.rem(n, 2)
    across = lax.rem(n + 2, narrow)
    sib = n + 1 - 2 * core
    sib_across = lax.rem(sib + 2, narrow)
    pair = own.shape[0]

    def place(plane, member):
        return x.at[plane, pl.ds(member * pair + 1, pair)]

    o_0, o_1 = jnp.where(far, across, n), jnp.where(far, n, across)
    oc_0, oc_1 = jnp.where(far, sib_across, sib), jnp.where(far, sib, sib_across)
    copies = [
        (None, own, place(1, n)),
        (None, other, place(1, across)),
        (None, g_c.at[0], place(1, sib)),
        (None, g_c.at[1], place(1, sib_across)),
        (None, r_e.at[0], place(plane_e, n)),
        (None, r_e.at[1], place(plane_e, across)),
        (None, e_c.at[0], place(plane_e, sib)),
        (None, e_c.at[1], place(plane_e, sib_across)),
        (has_o, r_o.at[0], place(plane_o, o_0)),
        (has_o, r_o.at[1], place(plane_o, o_1)),
        (has_o, o_c.at[0], place(plane_o, oc_0)),
        (has_o, o_c.at[1], place(plane_o, oc_1)),
    ]
    start_copies(copies, sems)
    rows = narrow * pair
    for p in range(3):
        x[p, 0] = jnp.zeros(x.shape[2:], BF16)
        x[p, rows + 1] = jnp.zeros(x.shape[2:], BF16)

    @pl.when(jnp.logical_not(has_o))
    def _():
        x[plane_o] = jnp.zeros(x.shape[1:], BF16)

    cells = own.shape[2] // 2
    lane = lax.broadcasted_iota(jnp.int32, (128, 2 * cells), 1)
    first = lambda v: (v == 0) | (v == cells)
    final = lambda v: (v == cells - 1) | (v == 2 * cells - 1)
    wait_copies(copies, sems)
    for j in range(rows // 2):
        stack = jnp.concatenate(
            [x[a, 2 * j : 2 * j + 4].reshape(256, 2 * cells) for a in range(3)], axis=0
        )
        acc = jnp.dot(t_d[...], stack, preferred_element_type=F32)
        both = shifted_sum(acc, lane, first, final)
        primal, tangent = activate(both[:, :cells], both[:, cells:])
        out_f[0, 2 * j : 2 * j + 2] = primal.reshape(2, 64, cells)
        out_t[0, 2 * j : 2 * j + 2] = tangent.reshape(2, 64, cells)


def call(body, outs, in_specs, out_specs, scratch, flops=0, nbytes=0):
    return pl.pallas_call(
        body,
        out_shape=[jax.ShapeDtypeStruct(s, BF16) for s in outs],
        in_specs=in_specs,
        out_specs=out_specs,
        scratch_shapes=scratch,
        compiler_params=pltpu.CompilerParams(vmem_limit_bytes=32 * 1024 * 1024),
        cost_estimate=pl.CostEstimate(flops=flops, bytes_accessed=nbytes, transcendentals=0),
    )


def local(wide, narrow, volume, volume_tangent, shallow_weight, deep_weight):
    planes, rows, chans, cells = volume.shape
    n = lax.axis_index("narrow")

    def swap(v, kind, route):
        return lax.ppermute(v, BOTH, exchange(wide, narrow, kind, route))

    face, edge, corner = (2, rows, chans, cells), (2, planes, chans, cells), (2, chans, cells)
    s_o, s_e, s_c, s_m, s_do, s_de = call(
        slices_kernel, [face, face, edge, edge, corner, corner], [ANY] * 2, [ANY] * 6,
        [pltpu.SemaphoreType.DMA((12,))], nbytes=2 << 20,
    )(volume, volume_tangent)
    r_o = swap(s_o, "O", "same")
    d_o = swap(s_do, "O", "mirror")
    r_e = swap(s_e, "E", "same")
    d_e = swap(s_de, "E", "mirror")
    r_c = swap(s_c, "", "core")
    r_m = swap(s_m, "", "mirror")
    band = (384, 768)
    t_s, t_d = call(
        weights_kernel, [band, band], [VMEM, ANY], [VMEM, VMEM],
        [
            pltpu.VMEM((3, 3, 3, 64, 128), BF16),
            pltpu.VMEM((9, 320, 64), BF16),
            pltpu.VMEM((9, 320, 128), BF16),
            pltpu.SemaphoreType.DMA,
        ],
        flops=10**8, nbytes=2 << 20,
    )(shallow_weight, deep_weight)
    row_c = jnp.where(n % 2 == 0, rows - 1, 0)
    c_e = swap(lax.dynamic_index_in_dim(r_e, row_c, 1, keepdims=False), "", "core")
    c_o = swap(lax.dynamic_index_in_dim(r_o, row_c, 1, keepdims=False), "", "core")
    skip_f, skip_t, pooled = call(
        functools.partial(shallow_kernel, wide, narrow),
        [volume.shape, volume.shape, (rows // 2, chans, cells)],
        [ANY] * 10 + [VMEM], [VMEM] * 3,
        [pltpu.VMEM((2, planes + 2, rows + 2, chans, cells), BF16), pltpu.SemaphoreType.DMA((18,))],
        flops=12 * 10**8, nbytes=4 << 20,
    )(volume, volume_tangent, r_o, r_e, r_c, r_m, c_o, c_e, d_o, d_e, t_s)
    other = swap(pooled, "", "across")
    group = jnp.stack([pooled, other])
    o2 = swap(group, "O", "near")
    e2 = swap(group, "E", "same")
    g_c = swap(group, "", "core")
    e_c = swap(e2, "", "core")
    o_c = swap(o2, "", "core")
    deep_shape = (1, rows // 2 * narrow, 64, cells // 2)
    deep_f, deep_t = call(
        functools.partial(deep_kernel, wide, narrow),
        [deep_shape, deep_shape],
        [ANY] * 7 + [VMEM], [VMEM] * 2,
        [
            pltpu.VMEM((3, rows // 2 * narrow + 2, chans, cells), BF16),
            pltpu.SemaphoreType.DMA((12,)),
        ],
        flops=6 * 10**8, nbytes=3 << 20,
    )(pooled, other, g_c, o2, e2, o_c, e_c, t_d)
    return skip_f, skip_t, deep_f, deep_t


def solution(mesh):
    wide, narrow = mesh.shape["wide"], mesh.shape["narrow"]
    in_specs = (P("wide", "narrow", None, None), P("wide", "narrow", None, None), P(), P())
    out_specs = (
        P("wide", "narrow", None, None),
        P("wide", "narrow", None, None),
        P("wide", None, "narrow", None),
        P("wide", None, "narrow", None),
    )
    return jax.shard_map(
        functools.partial(local, wide, narrow), mesh=mesh, in_specs=in_specs, out_specs=out_specs,
        check_vma=False,
    )
```

```python
import functools

import jax
import jax.numpy as jnp
from jax import lax
from jax.experimental import pallas as pl
from jax.experimental.pallas import tpu as pltpu
from jax.sharding import PartitionSpec as P

BOTH = ("wide", "narrow")
BF16 = jnp.bfloat16
F32 = jnp.float32
ANY = pl.BlockSpec(memory_space=pl.ANY)
VMEM = pl.BlockSpec(memory_space=pltpu.VMEM)
HBM = pl.BlockSpec(memory_space=pltpu.HBM)


def exchange(wide, narrow, kind, route):
    pairs = []
    for w in range(wide):
        for n in range(narrow):
            if kind == "E":
                pw = w ^ 1
            elif kind == "O":
                pw = w + 1 if w % 2 else w - 1
            else:
                pw = w
            if not 0 <= pw < wide:
                pw, pn = w, n ^ 1
            elif route == "same" or (route == "near" and min(w, pw) != wide // 2 - 1):
                pn = n
            elif route == "core":
                pn = n ^ 1
            elif route == "mirror":
                pn = narrow - 1 - n
            else:
                pn = n ^ 2
            pairs.append((w * narrow + n, pw * narrow + pn))
    return pairs


def run_copies(copies, sems):
    started = [pltpu.make_async_copy(src, dst, sems.at[k]) for k, (src, dst) in enumerate(copies)]
    for copy in started:
        copy.start()

    def wait():
        for copy in started:
            copy.wait()

    return wait


def slices_kernel(vol, tan, s_o, s_e, s_c, s_m, sems):
    w, n = lax.axis_index("wide"), lax.axis_index("narrow")
    odd = lax.rem(w, 2)
    last = vol.shape[1] - 1
    row_c = jnp.where(lax.rem(n, 2) == 0, last, 0)
    row_m = jnp.where(n < 2, last, 0)
    copies = []
    for t, src in enumerate((vol, tan)):
        copies += [
            (src.at[odd], s_o.at[t]),
            (src.at[1 - odd], s_e.at[t]),
            (src.at[:, row_c], s_c.at[:, t]),
            (src.at[:, row_m], s_m.at[:, t]),
        ]
    run_copies(copies, sems)()


def weights_kernel(sw, dw, t_s, t_d, dw_half, sw_all, band, dband, sem):
    n = lax.axis_index("narrow")
    shallow = pltpu.make_async_copy(sw, sw_all, sem.at[0])
    deep = pltpu.make_async_copy(
        dw.at[:, :, :, :, pl.ds(pl.multiple_of((n // 2) * 128, 128), 128)], dw_half, sem.at[1]
    )
    shallow.start()
    deep.start()
    band[...] = jnp.zeros_like(band)
    dband[...] = jnp.zeros_like(dband)
    nt = (((1,), (1,)), ((), ()))

    def build(source, scratch, pick, out):
        for a in range(3):
            for c in range(3):
                for b in range(3):
                    scratch[a * 3 + c, 64 * (b + 1) : 64 * (b + 2), :] = source[a, b, c]
                for r in range(2):
                    rows = scratch[a * 3 + c, 64 * (1 - r) : 64 * (1 - r) + 256, :]
                    placed = lax.dot_general(pick, rows, nt, preferred_element_type=F32)
                    out[a, c * 128 + r * 64 : c * 128 + r * 64 + 64, :] = placed.astype(BF16)

    def selector(width, shift):
        row = lax.broadcasted_iota(jnp.int32, (64, width), 0)
        col = lax.broadcasted_iota(jnp.int32, (64, width), 1)
        return jnp.where(col == row + shift, 1.0, 0.0).astype(BF16)

    shallow.wait()
    build(sw_all, band, selector(64, 0), t_s)
    deep.wait()
    build(dw_half, dband, selector(128, 64 * lax.rem(n, 2)), t_d)


def shifted_sum(acc, lane, first, final):
    left = pltpu.roll(acc[0:128], 1, 1)
    right = pltpu.roll(acc[256:384], acc.shape[1] - 1, 1)
    return acc[128:256] + jnp.where(first(lane), 0.0, left) + jnp.where(final(lane), 0.0, right)


def activate(pre, dot):
    s = 0.5 * jnp.tanh(0.5 * pre) + 0.5
    primal = (pre * s).astype(BF16)
    tangent = (s * (1.0 + pre * (1.0 - s)) * dot).astype(BF16)
    return primal, tangent


def pair_matrix(cells):
    source = lax.broadcasted_iota(jnp.int32, (cells, cells // 2), 0)
    target = lax.broadcasted_iota(jnp.int32, (cells, cells // 2), 1)
    return jnp.where(source // 2 == target, 0.125, 0.0).astype(BF16)


def pool_plane(out, pairing):
    halves = []
    for value in out:
        half = jnp.dot(value, pairing, preferred_element_type=F32)
        halves.append(half[0:64] + half[64:128])
    return jnp.concatenate(halves, axis=1)


def shallow_lanes(cells):
    lane = lax.broadcasted_iota(jnp.int32, (128, cells), 1)
    return lane, (lambda v: v == 0), (lambda v: v == cells - 1)


def row_windows(face, core_row, far_row, n, narrow):
    rows, chans, cells = face.shape
    far_row = jnp.where((n > 0) & (n < narrow - 1), far_row, jnp.zeros_like(far_row))
    even = lax.rem(n, 2) == 0
    top, bottom = jnp.where(even, far_row, core_row), jnp.where(even, core_row, far_row)
    flat = face.reshape(rows * chans, cells)
    return (
        jnp.concatenate([top, flat[: 3 * chans]], axis=0),
        jnp.concatenate([flat[chans:], bottom], axis=0),
    )


def own_kernel(narrow, vol, tan, r_c, r_m, t_s, part, x, sems):
    n = lax.axis_index("narrow")
    cells = vol.shape[3]
    run_copies([(vol, x.at[0]), (tan, x.at[1])], sems)()
    lane, first, final = shallow_lanes(cells)
    for t in range(2):
        stacks = [row_windows(x[t, p], r_c[p, t], r_m[p, t], n, narrow) for p in range(2)]
        for win in range(2):
            stack = jnp.concatenate([stacks[0][win], stacks[1][win]], axis=0)
            for q in range(2):
                taps = jnp.concatenate([t_s[1 - q], t_s[2 - q]], axis=1)
                acc = jnp.dot(taps, stack, preferred_element_type=F32)
                part[q, t, win] = shifted_sum(acc, lane, first, final)


def finish_plane(narrow, q, taps, face, rim, part, emit):
    n = lax.axis_index("narrow")
    cells = face.shape[3]
    lane, first, final = shallow_lanes(cells)
    pairing = pair_matrix(cells)
    stacks = [row_windows(face[t], rim[0, t], rim[1, t], n, narrow) for t in range(2)]
    for win in range(2):
        pre = []
        for t in range(2):
            acc = jnp.dot(taps, stacks[t][win], preferred_element_type=F32)
            pre.append(part[q, t, win] + shifted_sum(acc, lane, first, final))
        out = activate(*pre)
        emit(win, [v.reshape(2, 64, cells) for v in out], pool_plane(out, pairing))


def near_kernel(narrow, r_e, x_e, t_s, part, skip_f, skip_t, pool_part):
    odd = lax.rem(lax.axis_index("wide"), 2)

    def emit(win, out, pool):
        for t, ref in enumerate((skip_f, skip_t)):
            ref[2 * win : 2 * win + 2] = out[t]
        pool_part[win] = pool

    finish_plane(narrow, 1 - odd, t_s[2 - 2 * odd], r_e, x_e, part, emit)


def far_kernel(wide, narrow, r_o, x_o, t_s, part, pool_part, skip_f, skip_t, pooled):
    w = lax.axis_index("wide")
    odd = lax.rem(w, 2)

    def emit(win, out, pool):
        for t, ref in enumerate((skip_f, skip_t)):
            ref[2 * win : 2 * win + 2] = out[t]
        pooled[win] = (pool_part[win] + pool).astype(BF16)

    taps = t_s[2 * odd]
    taps = jnp.where((w > 0) & (w < wide - 1), taps, jnp.zeros_like(taps))
    finish_plane(narrow, odd, taps, r_o, x_o, part, emit)


def deep_lanes(cells):
    lane = lax.broadcasted_iota(jnp.int32, (128, 2 * cells), 1)
    first = lambda v: (v == 0) | (v == cells)
    final = lambda v: (v == cells - 1) | (v == 2 * cells - 1)
    return lane, first, final


def gather_rows(x, mine, sibling, far, narrow):
    n = lax.axis_index("narrow")
    sib = n + 1 - 2 * lax.rem(n, 2)
    pair = mine.shape[1]
    x[0] = jnp.zeros(x.shape[1:], BF16)
    x[narrow * pair + 1] = jnp.zeros(x.shape[1:], BF16)
    for source, member in ((mine, n), (sibling, sib)):
        for k in range(2):
            owner = lax.rem(member + 2 * k, narrow)
            if far is not None:
                owner = jnp.where(far, lax.rem(member + 2 - 2 * k, narrow), owner)
            x[pl.ds(owner * pair + 1, pair)] = source[k]


def deep_sum(x, taps, j, lane, first, final):
    stack = x[2 * j : 2 * j + 4].reshape(256, x.shape[2])
    acc = jnp.dot(taps, stack, preferred_element_type=F32)
    return shifted_sum(acc, lane, first, final)


def deep_own_kernel(narrow, group, g_c, t_d, near_f, near_t, far_f, far_t, part, order, skip_f, skip_t,
                    x, sems):
    odd = lax.rem(lax.axis_index("wide"), 2)
    wait = run_copies(
        [
            (near_f, skip_f.at[1 - odd]),
            (near_t, skip_t.at[1 - odd]),
            (far_f, skip_f.at[odd]),
            (far_t, skip_t.at[odd]),
        ],
        sems,
    )
    order[...] = jnp.zeros_like(order)
    gather_rows(x, group, g_c, None, narrow)
    lanes = deep_lanes(x.shape[2] // 2)
    for j in range(part.shape[0]):
        part[j] = deep_sum(x, t_d[1], j, *lanes)
    wait()


def deep_near_kernel(narrow, r_e, e_c, t_d, part, total, x):
    odd = lax.rem(lax.axis_index("wide"), 2)
    gather_rows(x, r_e, e_c, None, narrow)
    lanes = deep_lanes(x.shape[2] // 2)
    taps = t_d[2 - 2 * odd]
    for j in range(part.shape[0]):
        total[j] = part[j] + deep_sum(x, taps, j, *lanes)


def deep_far_kernel(wide, narrow, r_o, o_c, t_d, part, out_f, out_t, x):
    w = lax.axis_index("wide")
    cells = x.shape[2] // 2
    far = (w == wide // 2 - 1) | (w == wide // 2)
    gather_rows(x, r_o, o_c, far, narrow)
    lanes = deep_lanes(cells)
    taps = t_d[2 * lax.rem(w, 2)]
    taps = jnp.where((w > 0) & (w < wide - 1), taps, jnp.zeros_like(taps))
    for j in range(part.shape[0]):
        both = part[j] + deep_sum(x, taps, j, *lanes)
        primal, tangent = activate(both[:, :cells], both[:, cells:])
        out_f[0, 2 * j : 2 * j + 2] = primal.reshape(2, 64, cells)
        out_t[0, 2 * j : 2 * j + 2] = tangent.reshape(2, 64, cells)


def call(body, outs, in_specs, out_specs, scratch=()):
    return pl.pallas_call(
        body,
        out_shape=[o if hasattr(o, "dtype") else jax.ShapeDtypeStruct(o, BF16) for o in outs],
        in_specs=in_specs,
        out_specs=out_specs,
        scratch_shapes=list(scratch),
        compiler_params=pltpu.CompilerParams(vmem_limit_bytes=32 * 1024 * 1024),
        cost_estimate=pl.CostEstimate(flops=0, bytes_accessed=0, transcendentals=0),
    )


def local(wide, narrow, volume, volume_tangent, shallow_weight, deep_weight):
    planes, rows, chans, cells = volume.shape
    volume, volume_tangent, shallow_weight, deep_weight = (
        pltpu.with_memory_space_constraint(v, pltpu.HBM)
        for v in (volume, volume_tangent, shallow_weight, deep_weight)
    )
    odd = lax.axis_index("wide") % 2
    dma = pltpu.SemaphoreType.DMA

    def swap(v, kind, route):
        return lax.ppermute(v, BOTH, exchange(wide, narrow, kind, route))

    def full(*shape):
        return jax.ShapeDtypeStruct(shape, F32)

    face, edge = (2, rows, chans, cells), (planes, 2, chans, cells)
    s_o, s_e, s_c, s_m = call(
        slices_kernel, [face, face, edge, edge], [HBM] * 2, [ANY] * 4, [dma((8,))]
    )(volume, volume_tangent)
    r_o = swap(s_o, "O", "same")
    r_e = swap(s_e, "E", "same")
    r_c = swap(s_c, "", "core")
    r_m = swap(s_m, "", "mirror")
    rim = jnp.stack([r_c, r_m])
    x_o = swap(lax.dynamic_index_in_dim(rim, odd, 1, keepdims=False), "O", "same")
    x_e = swap(lax.dynamic_index_in_dim(rim, 1 - odd, 1, keepdims=False), "E", "same")
    band = (3, 384, 256)
    t_s, t_d = call(
        weights_kernel, [band, band], [HBM] * 2, [VMEM, VMEM],
        [
            pltpu.VMEM((3, 3, 3, 64, 128), BF16),
            pltpu.VMEM((3, 3, 3, 64, 64), BF16),
            pltpu.VMEM((9, 320, 64), BF16),
            pltpu.VMEM((9, 320, 128), BF16),
            dma((2,)),
        ],
    )(shallow_weight, deep_weight)
    wins = rows // 2
    (part,) = call(
        functools.partial(own_kernel, narrow),
        [full(planes, 2, wins, 128, cells)], [HBM] * 2 + [VMEM] * 3, [VMEM],
        [pltpu.VMEM((2, planes, rows, chans, cells), BF16), dma((2,))],
    )(volume, volume_tangent, r_c, r_m, t_s)
    plane = (rows, chans, cells)
    near_f, near_t, pool_part = call(
        functools.partial(near_kernel, narrow),
        [plane, plane, full(wins, chans, cells)], [VMEM] * 4, [VMEM] * 3,
    )(r_e, x_e, t_s, part)
    far_f, far_t, pooled = call(
        functools.partial(far_kernel, wide, narrow),
        [plane, plane, (wins, chans, cells)], [VMEM] * 5, [VMEM] * 3,
    )(r_o, x_o, t_s, part, pool_part)
    other = swap(pooled, "", "across")
    group = jnp.stack([pooled, other])
    o2 = swap(group, "O", "near")
    e2 = swap(group, "E", "same")
    g_c = swap(group, "", "core")
    deep_rows = wins * narrow
    sums = full(deep_rows // 2, 128, cells)
    gathered = pltpu.VMEM((deep_rows + 2, chans, cells), BF16)
    part_d, order, skip_f, skip_t = call(
        functools.partial(deep_own_kernel, narrow),
        [sums, (chans, cells), volume.shape, volume.shape],
        [VMEM] * 7, [VMEM, VMEM, HBM, HBM], [gathered, dma((4,))],
    )(group, g_c, t_d, near_f, near_t, far_f, far_t)
    e_c = swap(e2, "", "core")
    o_c = swap(o2 + order, "", "core")
    (total_d,) = call(
        functools.partial(deep_near_kernel, narrow), [sums], [VMEM] * 4, [VMEM], [gathered]
    )(e2, e_c, t_d, part_d)
    deep_shape = (1, deep_rows, 64, cells // 2)
    deep_f, deep_t = call(
        functools.partial(deep_far_kernel, wide, narrow),
        [deep_shape, deep_shape], [VMEM] * 4, [VMEM] * 2, [gathered],
    )(o2, o_c, t_d, total_d)
    return skip_f, skip_t, deep_f, deep_t


def solution(mesh):
    wide, narrow = mesh.shape["wide"], mesh.shape["narrow"]
    in_specs = (P("wide", "narrow", None, None), P("wide", "narrow", None, None), P(), P())
    out_specs = (
        P("wide", "narrow", None, None),
        P("wide", "narrow", None, None),
        P("wide", None, "narrow", None),
        P("wide", None, "narrow", None),
    )
    return jax.shard_map(
        functools.partial(local, wide, narrow), mesh=mesh, in_specs=in_specs, out_specs=out_specs,
        check_vma=False,
    )
```

```python
import functools

import jax
import jax.numpy as jnp
from jax import lax
from jax.experimental import pallas as pl
from jax.experimental.pallas import tpu as pltpu
from jax.sharding import PartitionSpec as P

BOTH = ("wide", "narrow")
PAD = 16
BF16 = jnp.bfloat16
F32 = jnp.float32
ANY = pl.BlockSpec(memory_space=pl.ANY)
VMEM = pl.BlockSpec(memory_space=pltpu.VMEM)
HBM = pl.BlockSpec(memory_space=pltpu.HBM)


def exchange(wide, narrow, kind, route):
    pairs = []
    for w in range(wide):
        for n in range(narrow):
            if kind == "E":
                pw = w ^ 1
            elif kind == "O":
                pw = w + 1 if w % 2 else w - 1
            else:
                pw = w
            if route == "mirror" and not 0 <= pw < wide:
                pw = w
            if not 0 <= pw < wide:
                pw, pn = w, n ^ 1
            elif route == "same" or (route == "near" and min(w, pw) != wide // 2 - 1):
                pn = n
            elif route == "core":
                pn = n ^ 1
            elif route == "mirror" and 0 < n < narrow - 1:
                pn = narrow - 1 - n
            elif route == "mirror":
                if wide % 8 == 0 and (w | 4) % (wide // 2) != wide // 2 - 1:
                    pw, pn = w ^ 4, n
                else:
                    pw, pn = (w + wide // 2) % wide, narrow - 1 - n
            else:
                pn = n ^ 2
            pairs.append((w * narrow + n, pw * narrow + pn))
    return pairs


def run_copies(copies, sems):
    started = [pltpu.make_async_copy(src, dst, sems.at[k]) for k, (src, dst) in enumerate(copies)]
    for copy in started:
        copy.start()

    def wait():
        for copy in started:
            copy.wait()

    return wait


def slices_kernel(vol, tan, s_o, s_e, s_c, s_m, sems):
    w, n = lax.axis_index("wide"), lax.axis_index("narrow")
    odd = lax.rem(w, 2)
    last = vol.shape[1] - 1
    row_c = jnp.where(lax.rem(n, 2) == 0, last, 0)
    row_m = jnp.where(n < 2, last, 0)
    copies = []
    for t, src in enumerate((vol, tan)):
        copies += [
            (src.at[odd], s_o.at[t]),
            (src.at[1 - odd], s_e.at[t]),
            (src.at[:, row_c], s_c.at[:, t]),
            (src.at[:, row_m], s_m.at[:, t]),
        ]
    run_copies(copies, sems)()


def weights_kernel(vol, tan, sw, dw, t_s, t_d, own, dw_half, sw_all, band, dband, sem, sems):
    n = lax.axis_index("narrow")
    wait = run_copies([(vol, own.at[0]), (tan, own.at[1])], sems)
    shallow = pltpu.make_async_copy(sw, sw_all, sem.at[0])
    deep = pltpu.make_async_copy(
        dw.at[:, :, :, :, pl.ds(pl.multiple_of((n // 2) * 128, 128), 128)], dw_half, sem.at[1]
    )
    shallow.start()
    deep.start()
    band[...] = jnp.zeros_like(band)
    dband[...] = jnp.zeros_like(dband)
    nt = (((1,), (1,)), ((), ()))

    def build(source, scratch, pick, out):
        for a in range(3):
            for c in range(3):
                for b in range(3):
                    scratch[a * 3 + c, 64 * (b + 1) : 64 * (b + 2), :] = source[a, b, c]
                for r in range(2):
                    rows = scratch[a * 3 + c, 64 * (1 - r) : 64 * (1 - r) + 256, :]
                    placed = lax.dot_general(pick, rows, nt, preferred_element_type=F32)
                    out[a, c * 128 + r * 64 : c * 128 + r * 64 + 64, :] = placed.astype(BF16)

    def selector(width, shift):
        row = lax.broadcasted_iota(jnp.int32, (64, width), 0)
        col = lax.broadcasted_iota(jnp.int32, (64, width), 1)
        return jnp.where(col == row + shift, 1.0, 0.0).astype(BF16)

    shallow.wait()
    build(sw_all, band, selector(64, 0), t_s)
    deep.wait()
    build(dw_half, dband, selector(128, 64 * lax.rem(n, 2)), t_d)
    wait()


def shifted_sum(acc, lane, first, final):
    left = pltpu.roll(acc[0:128], 1, 1)
    right = pltpu.roll(acc[256:384], acc.shape[1] - 1, 1)
    return acc[128:256] + jnp.where(first(lane), 0.0, left) + jnp.where(final(lane), 0.0, right)


def activate(pre, dot):
    s = 0.5 * jnp.tanh(0.5 * pre) + 0.5
    primal = (pre * s).astype(BF16)
    tangent = (s * (1.0 + pre * (1.0 - s)) * dot).astype(BF16)
    return primal, tangent


def pair_matrix(cells):
    source = lax.broadcasted_iota(jnp.int32, (cells, cells // 2), 0)
    target = lax.broadcasted_iota(jnp.int32, (cells, cells // 2), 1)
    return jnp.where(source // 2 == target, 0.125, 0.0).astype(BF16)


def pool_plane(out, pairing):
    halves = []
    for value in out:
        half = jnp.dot(value, pairing, preferred_element_type=F32)
        halves.append(half[0:64] + half[64:128])
    return jnp.concatenate(halves, axis=1)


def shallow_lanes(cells):
    lane = lax.broadcasted_iota(jnp.int32, (128, cells), 1)
    return lane, (lambda v: v == 0), (lambda v: v == cells - 1)


def row_windows(face, core_row, far_row, n, narrow):
    rows, chans, cells = face.shape
    far_row = jnp.where((n > 0) & (n < narrow - 1), far_row, jnp.zeros_like(far_row))
    even = lax.rem(n, 2) == 0
    top, bottom = jnp.where(even, far_row, core_row), jnp.where(even, core_row, far_row)
    flat = face.reshape(rows * chans, cells)
    return (
        jnp.concatenate([top, flat[: 3 * chans]], axis=0),
        jnp.concatenate([flat[chans:], bottom], axis=0),
    )


def edge_kernel(face, *rest):
    row_c, row_m = rest[-2:]
    n = lax.axis_index("narrow")
    last = face.shape[1] - 1
    for t in range(2):
        row_c[t] = jnp.where(lax.rem(n, 2) == 0, face[t, last], face[t, 0])
        row_m[t, 0 : face.shape[2]] = jnp.where(n < 2, face[t, last], face[t, 0])
        row_m[t, face.shape[2] :] = jnp.zeros((PAD, face.shape[3]), BF16)


def own_kernel(narrow, x, r_c, r_m, t_s, part):
    n = lax.axis_index("narrow")
    cells = x.shape[4]
    lane, first, final = shallow_lanes(cells)
    for t in range(2):
        stacks = [row_windows(x[t, p], r_c[p, t], r_m[p, t], n, narrow) for p in range(2)]
        for win in range(2):
            stack = jnp.concatenate([stacks[0][win], stacks[1][win]], axis=0)
            for q in range(2):
                taps = jnp.concatenate([t_s[1 - q], t_s[2 - q]], axis=1)
                acc = jnp.dot(taps, stack, preferred_element_type=F32)
                part[q, t, win] = shifted_sum(acc, lane, first, final)


def finish_plane(narrow, q, taps, face, core_row, far_row, part, emit):
    n = lax.axis_index("narrow")
    chans, cells = face.shape[2:]
    lane, first, final = shallow_lanes(cells)
    pairing = pair_matrix(cells)
    stacks = [row_windows(face[t], core_row[t], far_row[t, 0:chans], n, narrow) for t in range(2)]
    for win in range(2):
        pre = []
        for t in range(2):
            acc = jnp.dot(taps, stacks[t][win], preferred_element_type=F32)
            pre.append(part[q, t, win] + shifted_sum(acc, lane, first, final))
        out = activate(*pre)
        emit(win, [v.reshape(2, 64, cells) for v in out], pool_plane(out, pairing))


def near_kernel(narrow, r_e, c_e, m_e, t_s, part, skip_f, skip_t, pool_part):
    odd = lax.rem(lax.axis_index("wide"), 2)

    def emit(win, out, pool):
        for t, ref in enumerate((skip_f, skip_t)):
            ref[2 * win : 2 * win + 2] = out[t]
        pool_part[win] = pool

    finish_plane(narrow, 1 - odd, t_s[2 - 2 * odd], r_e, c_e, m_e, part, emit)


def far_kernel(wide, narrow, r_o, c_o, m_o, t_s, part, pool_part, skip_f, skip_t, pooled):
    w = lax.axis_index("wide")
    odd = lax.rem(w, 2)

    def emit(win, out, pool):
        for t, ref in enumerate((skip_f, skip_t)):
            ref[2 * win : 2 * win + 2] = out[t]
        pooled[win] = (pool_part[win] + pool).astype(BF16)

    taps = t_s[2 * odd]
    taps = jnp.where((w > 0) & (w < wide - 1), taps, jnp.zeros_like(taps))
    finish_plane(narrow, odd, taps, r_o, c_o, m_o, part, emit)


def deep_lanes(cells):
    lane = lax.broadcasted_iota(jnp.int32, (128, 2 * cells), 1)
    first = lambda v: (v == 0) | (v == cells)
    final = lambda v: (v == cells - 1) | (v == 2 * cells - 1)
    return lane, first, final


def gather_rows(x, parts, far, narrow):
    n = lax.axis_index("narrow")
    sib = n + 1 - 2 * lax.rem(n, 2)
    pair = parts[0].shape[0]
    x[0] = jnp.zeros(x.shape[1:], BF16)
    x[narrow * pair + 1] = jnp.zeros(x.shape[1:], BF16)
    for k, source in enumerate(parts):
        member = n if k < 2 else sib
        owner = lax.rem(member + 2 * (k % 2), narrow)
        if far is not None:
            owner = jnp.where(far, lax.rem(member + 2 - 2 * (k % 2), narrow), owner)
        x[pl.ds(owner * pair + 1, pair)] = source[...]


def deep_sum(x, taps, j, lane, first, final):
    stack = x[2 * j : 2 * j + 4].reshape(256, x.shape[2])
    acc = jnp.dot(taps, stack, preferred_element_type=F32)
    return shifted_sum(acc, lane, first, final)


def deep_near_kernel(narrow, own, across, own_c, across_c, e, e_across, e_c, e_across_c, t_d, near_f, near_t, far_f, far_t,
                     total, skip_f, skip_t, x, y, sems):
    odd = lax.rem(lax.axis_index("wide"), 2)
    wait = run_copies(
        [
            (near_f, skip_f.at[1 - odd]),
            (near_t, skip_t.at[1 - odd]),
            (far_f, skip_f.at[odd]),
            (far_t, skip_t.at[odd]),
        ],
        sems,
    )
    gather_rows(x, (own, across, own_c, across_c), None, narrow)
    gather_rows(y, (e, e_across, e_c, e_across_c), None, narrow)
    cells = x.shape[2]
    lanes = deep_lanes(cells // 2)
    taps = jnp.concatenate([t_d[1], t_d[2 - 2 * odd]], axis=1)
    for j in range(total.shape[0]):
        stack = [v[2 * j : 2 * j + 4].reshape(256, cells) for v in (x, y)]
        acc = jnp.dot(taps, jnp.concatenate(stack, axis=0), preferred_element_type=F32)
        total[j] = shifted_sum(acc, *lanes)
    wait()


def deep_far_kernel(wide, narrow, o, o_across, o_c, o_across_c, t_d, part, out_f, out_t, x):
    w = lax.axis_index("wide")
    cells = x.shape[2] // 2
    far = (w == wide // 2 - 1) | (w == wide // 2)
    gather_rows(x, (o, o_across, o_c, o_across_c), far, narrow)
    lanes = deep_lanes(cells)
    taps = t_d[2 * lax.rem(w, 2)]
    taps = jnp.where((w > 0) & (w < wide - 1), taps, jnp.zeros_like(taps))
    for j in range(part.shape[0]):
        both = part[j] + deep_sum(x, taps, j, *lanes)
        primal, tangent = activate(both[:, :cells], both[:, cells:])
        out_f[0, 2 * j : 2 * j + 2] = primal.reshape(2, 64, cells)
        out_t[0, 2 * j : 2 * j + 2] = tangent.reshape(2, 64, cells)


def call(body, outs, in_specs, out_specs, scratch=()):
    return pl.pallas_call(
        body,
        out_shape=[o if hasattr(o, "dtype") else jax.ShapeDtypeStruct(o, BF16) for o in outs],
        in_specs=in_specs,
        out_specs=out_specs,
        scratch_shapes=list(scratch),
        compiler_params=pltpu.CompilerParams(vmem_limit_bytes=32 * 1024 * 1024),
        cost_estimate=pl.CostEstimate(flops=0, bytes_accessed=0, transcendentals=0),
    )


def local(wide, narrow, volume, volume_tangent, shallow_weight, deep_weight):
    planes, rows, chans, cells = volume.shape
    volume, volume_tangent, shallow_weight, deep_weight = (
        pltpu.with_memory_space_constraint(v, pltpu.HBM)
        for v in (volume, volume_tangent, shallow_weight, deep_weight)
    )
    dma = pltpu.SemaphoreType.DMA

    def swap(v, kind, route):
        return lax.ppermute(v, BOTH, exchange(wide, narrow, kind, route))

    def full(*shape):
        return jax.ShapeDtypeStruct(shape, F32)

    plane, edge = (rows, chans, cells), (planes, 2, chans, cells)
    s_o, s_e, s_c, s_m = call(
        slices_kernel, [(2,) + plane, (2,) + plane, edge, edge],
        [HBM] * 2, [ANY] * 4, [dma((8,))],
    )(volume, volume_tangent)
    r_o = swap(s_o, "O", "same")
    r_e = swap(s_e, "E", "same")
    r_c = swap(s_c, "", "core")
    r_m = swap(s_m, "", "mirror")
    band = (3, 384, 256)
    t_s, t_d, own = call(
        weights_kernel, [band, band, (2,) + volume.shape], [HBM] * 4, [VMEM, VMEM, ANY],
        [
            pltpu.VMEM((3, 3, 3, 64, 128), BF16),
            pltpu.VMEM((3, 3, 3, 64, 64), BF16),
            pltpu.VMEM((9, 320, 64), BF16),
            pltpu.VMEM((9, 320, 128), BF16),
            dma((2,)),
            dma((2,)),
        ],
    )(volume, volume_tangent, shallow_weight, deep_weight)
    wins = rows // 2
    (part,) = call(
        functools.partial(own_kernel, narrow),
        [full(planes, 2, wins, 128, cells)], [VMEM] * 4, [VMEM],
    )(own, r_c, r_m, t_s)
    corners = [(2, chans, cells), (2, chans + PAD, cells)]
    row_ec, row_em = call(edge_kernel, corners, [VMEM], [VMEM] * 2)(r_e)
    c_e, m_e = swap(row_ec, "", "core"), swap(row_em, "", "mirror")
    row_oc, row_om = call(edge_kernel, corners, [VMEM] * 3, [VMEM] * 2)(r_o, part, row_ec)
    c_o, m_o = swap(row_oc, "", "core"), swap(row_om, "", "mirror")
    near_f, near_t, pool_part = call(
        functools.partial(near_kernel, narrow),
        [plane, plane, full(wins, chans, cells)], [VMEM] * 5, [VMEM] * 3,
    )(r_e, c_e, m_e, t_s, part)
    far_f, far_t, pooled = call(
        functools.partial(far_kernel, wide, narrow),
        [plane, plane, (wins, chans, cells)], [VMEM] * 6, [VMEM] * 3,
    )(r_o, c_o, m_o, t_s, part, pool_part)
    o2 = swap(pooled, "O", "near")
    e2 = swap(pooled, "E", "same")
    across = swap(pooled, "", "across")
    e_across = swap(e2, "", "across")
    o_across = swap(o2, "", "across")
    own_c, across_c = swap(pooled, "", "core"), swap(across, "", "core")
    e_c, e_across_c = swap(e2, "", "core"), swap(e_across, "", "core")
    o_c, o_across_c = swap(o2, "", "core"), swap(o_across, "", "core")
    deep_rows = wins * narrow
    sums = full(deep_rows // 2, 128, cells)
    gathered = pltpu.VMEM((deep_rows + 2, chans, cells), BF16)
    total_d, skip_f, skip_t = call(
        functools.partial(deep_near_kernel, narrow),
        [sums, volume.shape, volume.shape],
        [VMEM] * 13, [VMEM, HBM, HBM], [gathered, gathered, dma((4,))],
    )(pooled, across, own_c, across_c, e2, e_across, e_c, e_across_c, t_d, near_f, near_t, far_f, far_t)
    deep_shape = (1, deep_rows, 64, cells // 2)
    deep_f, deep_t = call(
        functools.partial(deep_far_kernel, wide, narrow),
        [deep_shape, deep_shape], [VMEM] * 6, [VMEM] * 2, [gathered],
    )(o2, o_across, o_c, o_across_c, t_d, total_d)
    return skip_f, skip_t, deep_f, deep_t


def solution(mesh):
    wide, narrow = mesh.shape["wide"], mesh.shape["narrow"]
    in_specs = (P("wide", "narrow", None, None), P("wide", "narrow", None, None), P(), P())
    out_specs = (
        P("wide", "narrow", None, None),
        P("wide", "narrow", None, None),
        P("wide", None, "narrow", None),
        P("wide", None, "narrow", None),
    )
    return jax.shard_map(
        functools.partial(local, wide, narrow), mesh=mesh, in_specs=in_specs, out_specs=out_specs,
        check_vma=False,
    )
```

```python
import functools

import jax
import jax.numpy as jnp
from jax import lax
from jax.experimental import pallas as pl
from jax.experimental.pallas import tpu as pltpu
from jax.sharding import PartitionSpec as P

BOTH = ("wide", "narrow")
PAD = 16
BF16 = jnp.bfloat16
F32 = jnp.float32
ANY = pl.BlockSpec(memory_space=pl.ANY)
VMEM = pl.BlockSpec(memory_space=pltpu.VMEM)
HBM = pl.BlockSpec(memory_space=pltpu.HBM)


def exchange(wide, narrow, kind, route):
    pairs = []
    for w in range(wide):
        for n in range(narrow):
            if kind == "E":
                pw = w ^ 1
            elif kind == "O":
                pw = w + 1 if w % 2 else w - 1
            else:
                pw = w
            if route == "mirror" and not 0 <= pw < wide:
                pw = w
            if not 0 <= pw < wide:
                pw, pn = w, n ^ 1
            elif route == "same" or (route == "near" and min(w, pw) != wide // 2 - 1):
                pn = n
            elif route == "core":
                pn = n ^ 1
            elif route in ("mirror", "corner") and 0 < n < narrow - 1:
                pn = narrow - 1 - n
            elif route in ("mirror", "corner"):
                if wide % 8 == 0 and (route == "corner" or (w | 4) % (wide // 2) != wide // 2 - 1):
                    pw, pn = w ^ 4, n
                else:
                    pw, pn = (w + wide // 2) % wide, narrow - 1 - n
            else:
                pn = n ^ 2
            pairs.append((w * narrow + n, pw * narrow + pn))
    return pairs


def run_copies(copies, sems):
    started = [pltpu.make_async_copy(src, dst, sems.at[k]) for k, (src, dst) in enumerate(copies)]
    for copy in started:
        copy.start()

    def wait():
        for copy in started:
            copy.wait()

    return wait


def slices_kernel(vol, tan, s_o, s_e, s_c, s_m, sems):
    w, n = lax.axis_index("wide"), lax.axis_index("narrow")
    odd = lax.rem(w, 2)
    last = vol.shape[1] - 1
    row_c = jnp.where(lax.rem(n, 2) == 0, last, 0)
    row_m = jnp.where(n < 2, last, 0)
    copies = []
    for t, src in enumerate((vol, tan)):
        for plane, face in ((odd, s_o), (1 - odd, s_e)):
            for half in range(2):
                rows = pl.ds(2 * half, 2)
                copies.append((src.at[plane, rows], face.at[t, rows]))
        copies += [(src.at[:, row_c], s_c.at[:, t]), (src.at[:, row_m], s_m.at[:, t])]
    run_copies(copies, sems)()


def weights_kernel(vol, tan, sw, dw, t_s, t_d, own, dw_half, sw_all, band, dband, sem, sems):
    n = lax.axis_index("narrow")
    wait = run_copies([(vol, own.at[0]), (tan, own.at[1])], sems)
    shallow = pltpu.make_async_copy(sw, sw_all, sem.at[0])
    deep = pltpu.make_async_copy(
        dw.at[:, :, :, :, pl.ds(pl.multiple_of((n // 2) * 128, 128), 128)], dw_half, sem.at[1]
    )
    shallow.start()
    deep.start()
    band[...] = jnp.zeros_like(band)
    dband[...] = jnp.zeros_like(dband)
    nt = (((1,), (1,)), ((), ()))

    def build(source, scratch, pick, out):
        for a in range(3):
            for c in range(3):
                for b in range(3):
                    scratch[a * 3 + c, 64 * (b + 1) : 64 * (b + 2), :] = source[a, b, c]
                for r in range(2):
                    rows = scratch[a * 3 + c, 64 * (1 - r) : 64 * (1 - r) + 256, :]
                    placed = lax.dot_general(pick, rows, nt, preferred_element_type=F32)
                    out[a, c * 128 + r * 64 : c * 128 + r * 64 + 64, :] = placed.astype(BF16)

    def selector(width, shift):
        row = lax.broadcasted_iota(jnp.int32, (64, width), 0)
        col = lax.broadcasted_iota(jnp.int32, (64, width), 1)
        return jnp.where(col == row + shift, 1.0, 0.0).astype(BF16)

    shallow.wait()
    build(sw_all, band, selector(64, 0), t_s)
    deep.wait()
    build(dw_half, dband, selector(128, 64 * lax.rem(n, 2)), t_d)
    wait()


def shifted_sum(acc, lane, first, final):
    left = pltpu.roll(acc[0:128], 1, 1)
    right = pltpu.roll(acc[256:384], acc.shape[1] - 1, 1)
    return acc[128:256] + jnp.where(first(lane), 0.0, left) + jnp.where(final(lane), 0.0, right)


def activate(pre, dot):
    s = 0.5 * jnp.tanh(0.5 * pre) + 0.5
    primal = (pre * s).astype(BF16)
    tangent = (s * (1.0 + pre * (1.0 - s)) * dot).astype(BF16)
    return primal, tangent


def pair_matrix(cells):
    source = lax.broadcasted_iota(jnp.int32, (cells, cells // 2), 0)
    target = lax.broadcasted_iota(jnp.int32, (cells, cells // 2), 1)
    return jnp.where(source // 2 == target, 0.125, 0.0).astype(BF16)


def pool_plane(out, pairing):
    halves = [jnp.dot(value, pairing, preferred_element_type=F32) for value in out]
    return jnp.concatenate(halves, axis=1)


def shallow_lanes(cells):
    lane = lax.broadcasted_iota(jnp.int32, (128, cells), 1)
    return lane, (lambda v: v == 0), (lambda v: v == cells - 1)


def row_windows(face, core_row, far_row, n, narrow):
    rows, chans, cells = face.shape
    far_row = jnp.where((n > 0) & (n < narrow - 1), far_row, jnp.zeros_like(far_row))
    even = lax.rem(n, 2) == 0
    top, bottom = jnp.where(even, far_row, core_row), jnp.where(even, core_row, far_row)
    flat = face.reshape(rows * chans, cells)
    return (
        jnp.concatenate([top, flat[: 3 * chans]], axis=0),
        jnp.concatenate([flat[chans:], bottom], axis=0),
    )


def edge_kernel(face, *rest):
    row_c, row_m = rest[-2:]
    n = lax.axis_index("narrow")
    last = face.shape[1] - 1
    for t in range(2):
        for row, is_last in ((row_c, lax.rem(n, 2) == 0), (row_m, n < 2)):
            chans = face.shape[2]
            row[t, 0:chans] = jnp.where(is_last, face[t, last], face[t, 0])
            if row.shape[1] > chans:
                row[t, chans:] = jnp.zeros((row.shape[1] - chans, face.shape[3]), BF16)


def own_kernel(narrow, x, r_c, r_m, t_s, part):
    n = lax.axis_index("narrow")
    cells = x.shape[4]
    lane, first, final = shallow_lanes(cells)
    for t in range(2):
        stacks = [row_windows(x[t, p], r_c[p, t], r_m[p, t], n, narrow) for p in range(2)]
        for win in range(2):
            stack = jnp.concatenate([stacks[0][win], stacks[1][win]], axis=0)
            for q in range(2):
                taps = jnp.concatenate([t_s[1 - q], t_s[2 - q]], axis=1)
                acc = jnp.dot(taps, stack, preferred_element_type=F32)
                part[q, t, win] = shifted_sum(acc, lane, first, final)


def finish_plane(narrow, q, taps, face, core_row, far_row, part, emit):
    n = lax.axis_index("narrow")
    chans, cells = face.shape[2:]
    lane, first, final = shallow_lanes(cells)
    pairing = pair_matrix(cells)
    stacks = []
    for t in range(2):
        far = jnp.zeros((chans, cells), BF16) if far_row is None else far_row[t, 0:chans]
        stacks.append(row_windows(face[t], core_row[t, 0:chans], far, n, narrow))
    for win in range(2):
        pre = []
        for t in range(2):
            acc = jnp.dot(taps, stacks[t][win], preferred_element_type=F32)
            pre.append(part[q, t, win] + shifted_sum(acc, lane, first, final))
        out = activate(*pre)
        emit(win, pre, [v.reshape(2, 64, cells) for v in out], pool_plane(out, pairing))


def near_kernel(narrow, r_e, c_e, m_e, t_s, part, skip_f, skip_t, pool_part):
    odd = lax.rem(lax.axis_index("wide"), 2)

    def emit(win, pre, out, pool):
        for t, ref in enumerate((skip_f, skip_t)):
            ref[2 * win : 2 * win + 2] = out[t]
        pool_part[win] = pool[0:64] + pool[64:128]

    finish_plane(narrow, 1 - odd, t_s[2 - 2 * odd], r_e, c_e, m_e, part, emit)


def far_taps(wide, t_s):
    w = lax.axis_index("wide")
    taps = t_s[2 * lax.rem(w, 2)]
    return jnp.where((w > 0) & (w < wide - 1), taps, jnp.zeros_like(taps))


def far_kernel(wide, narrow, r_o, c_o, t_s, part, pool_part, skip_f, skip_t, pool_far, edge_pre):
    odd = lax.rem(lax.axis_index("wide"), 2)
    even_n = lax.rem(lax.axis_index("narrow"), 2) == 0

    def emit(win, pre, out, pool):
        for t, ref in enumerate((skip_f, skip_t)):
            ref[2 * win : 2 * win + 2] = out[t]
        none = jnp.zeros_like(pool[0:64])
        if win == 0:
            pool_far[0] = pool_part[0] + jnp.where(even_n, none, pool[0:64]) + pool[64:128]
            for t in range(2):
                edge_pre[t] = pre[t][0:64]
        else:
            pool_far[1] = pool_part[1] + pool[0:64] + jnp.where(even_n, pool[64:128], none)
            for t in range(2):
                edge_pre[t] = jnp.where(even_n, edge_pre[t], pre[t][64:128])

    finish_plane(narrow, odd, far_taps(wide, t_s), r_o, c_o, None, part, emit)


def edge_row_kernel(wide, narrow, m_o, t_s, edge_pre, pool_far, edge_f, edge_t, pooled):
    n = lax.axis_index("narrow")
    chans, cells = edge_pre.shape[1:]
    even_n = lax.rem(n, 2) == 0
    has_m = (n > 0) & (n < narrow - 1)
    lane, first, final = shallow_lanes(cells)
    taps = far_taps(wide, t_s)
    pre = []
    for t in range(2):
        row = m_o[t, 0:chans]
        row = jnp.where(has_m, row, jnp.zeros_like(row))
        none = jnp.zeros_like(row)
        stack = [jnp.where(even_n, row, none), none, none, jnp.where(even_n, none, row)]
        acc = jnp.dot(taps, jnp.concatenate(stack, axis=0), preferred_element_type=F32)
        both = shifted_sum(acc, lane, first, final)
        pre.append(edge_pre[t] + jnp.where(even_n, both[0:chans], both[chans:]))
    out = activate(*pre)
    edge_f[...], edge_t[...] = out
    pool = pool_plane(out, pair_matrix(cells))
    for win in range(2):
        mine = even_n if win == 0 else jnp.logical_not(even_n)
        pooled[win] = (pool_far[win] + jnp.where(mine, pool, jnp.zeros_like(pool))).astype(BF16)


def deep_lanes(cells):
    lane = lax.broadcasted_iota(jnp.int32, (128, 2 * cells), 1)
    first = lambda v: (v == 0) | (v == cells)
    final = lambda v: (v == cells - 1) | (v == 2 * cells - 1)
    return lane, first, final


def gather_rows(x, parts, far, narrow):
    n = lax.axis_index("narrow")
    sib = n + 1 - 2 * lax.rem(n, 2)
    pair = parts[0].shape[0]
    x[0] = jnp.zeros(x.shape[1:], BF16)
    x[narrow * pair + 1] = jnp.zeros(x.shape[1:], BF16)
    for k, source in enumerate(parts):
        member = n if k < 2 else sib
        owner = lax.rem(member + 2 * (k % 2), narrow)
        if far is not None:
            owner = jnp.where(far, lax.rem(member + 2 - 2 * (k % 2), narrow), owner)
        x[pl.ds(owner * pair + 1, pair)] = source[...]


def deep_sum(x, taps, j, lane, first, final):
    stack = x[2 * j : 2 * j + 4].reshape(256, x.shape[2])
    acc = jnp.dot(taps, stack, preferred_element_type=F32)
    return shifted_sum(acc, lane, first, final)


def deep_near_kernel(narrow, own, across, own_c, across_c, e, e_across, e_c, e_across_c, t_d, near_f, near_t,
                     far_f, far_t, edge_f, edge_t, total, skip_f, skip_t, x, y, sems):
    odd = lax.rem(lax.axis_index("wide"), 2)
    even_n = lax.rem(lax.axis_index("narrow"), 2) == 0
    last = far_f.shape[0] - 1
    edge, rest = jnp.where(even_n, 0, last), pl.ds(jnp.where(even_n, 1, 0), last)
    copies = []
    for near, far, row, skip in ((near_f, far_f, edge_f, skip_f), (near_t, far_t, edge_t, skip_t)):
        copies += [
            (near, skip.at[1 - odd]),
            (far.at[rest], skip.at[odd, rest]),
            (row, skip.at[odd, edge]),
        ]
    wait = run_copies(copies, sems)
    gather_rows(x, (own, across, own_c, across_c), None, narrow)
    gather_rows(y, (e, e_across, e_c, e_across_c), None, narrow)
    cells = x.shape[2]
    lanes = deep_lanes(cells // 2)
    taps = jnp.concatenate([t_d[1], t_d[2 - 2 * odd]], axis=1)
    for j in range(total.shape[0]):
        stack = [v[2 * j : 2 * j + 4].reshape(256, cells) for v in (x, y)]
        acc = jnp.dot(taps, jnp.concatenate(stack, axis=0), preferred_element_type=F32)
        total[j] = shifted_sum(acc, *lanes)
    wait()


def deep_far_kernel(wide, narrow, o, o_across, o_c, o_across_c, t_d, part, out_f, out_t, x, staged, sems):
    w = lax.axis_index("wide")
    cells = x.shape[2] // 2
    far = (w == wide // 2 - 1) | (w == wide // 2)
    gather_rows(x, (o, o_across, o_c, o_across_c), far, narrow)
    lanes = deep_lanes(cells)
    taps = far_taps(wide, t_d)
    waits = []
    for j in range(part.shape[0]):
        both = part[j] + deep_sum(x, taps, j, *lanes)
        out = activate(both[:, :cells], both[:, cells:])
        rows = pl.ds(2 * j, 2)
        copies = []
        for t, ref in enumerate((out_f, out_t)):
            staged[t, 2 * j : 2 * j + 2] = out[t].reshape(2, 64, cells)
            copies.append((staged.at[t, rows], ref.at[0, rows]))
        waits.append(run_copies(copies, sems.at[j]))
    for wait in waits:
        wait()


def call(body, outs, in_specs, out_specs, scratch=()):
    return pl.pallas_call(
        body,
        out_shape=[o if hasattr(o, "dtype") else jax.ShapeDtypeStruct(o, BF16) for o in outs],
        in_specs=in_specs,
        out_specs=out_specs,
        scratch_shapes=list(scratch),
        compiler_params=pltpu.CompilerParams(vmem_limit_bytes=32 * 1024 * 1024),
        cost_estimate=pl.CostEstimate(flops=0, bytes_accessed=0, transcendentals=0),
    )


def local(wide, narrow, volume, volume_tangent, shallow_weight, deep_weight):
    planes, rows, chans, cells = volume.shape
    volume, volume_tangent, shallow_weight, deep_weight = (
        pltpu.with_memory_space_constraint(v, pltpu.HBM)
        for v in (volume, volume_tangent, shallow_weight, deep_weight)
    )
    dma = pltpu.SemaphoreType.DMA

    def swap(v, kind, route):
        return lax.ppermute(v, BOTH, exchange(wide, narrow, kind, route))

    def full(*shape):
        return jax.ShapeDtypeStruct(shape, F32)

    plane, edge = (rows, chans, cells), (planes, 2, chans, cells)
    s_o, s_e, s_c, s_m = call(
        slices_kernel, [(2,) + plane, (2,) + plane, edge, edge],
        [HBM] * 2, [ANY] * 4, [dma((12,))],
    )(volume, volume_tangent)
    r_o = swap(s_o, "O", "same")
    r_e = swap(s_e, "E", "same")
    r_c = swap(s_c, "", "core")
    r_m = swap(s_m, "", "mirror")
    band = (3, 384, 256)
    t_s, t_d, own = call(
        weights_kernel, [band, band, (2,) + volume.shape], [HBM] * 4, [VMEM, VMEM, ANY],
        [
            pltpu.VMEM((3, 3, 3, 64, 128), BF16),
            pltpu.VMEM((3, 3, 3, 64, 64), BF16),
            pltpu.VMEM((9, 320, 64), BF16),
            pltpu.VMEM((9, 320, 128), BF16),
            dma((2,)),
            dma((2,)),
        ],
    )(volume, volume_tangent, shallow_weight, deep_weight)
    wins = rows // 2
    (part,) = call(
        functools.partial(own_kernel, narrow),
        [full(planes, 2, wins, 128, cells)], [VMEM] * 4, [VMEM],
    )(own, r_c, r_m, t_s)
    row_ec, row_em = call(edge_kernel, [(2, chans + 2 * PAD, cells)] * 2, [VMEM], [VMEM] * 2)(r_e)
    c_e, m_e = swap(row_ec, "", "core"), swap(row_em, "", "corner")
    row_oc, row_om = call(edge_kernel, [(2, chans, cells), (2, chans + PAD, cells)], [VMEM] * 3, [VMEM] * 2)(r_o, part, row_ec)
    c_o, m_o = swap(row_oc, "", "core"), swap(row_om, "", "corner")
    near_f, near_t, pool_part = call(
        functools.partial(near_kernel, narrow),
        [plane, plane, full(wins, chans, cells)], [VMEM] * 5, [VMEM] * 3,
    )(r_e, c_e, m_e, t_s, part)
    far_f, far_t, pool_far, edge_pre = call(
        functools.partial(far_kernel, wide, narrow),
        [plane, plane, full(wins, chans, cells), full(2, chans, cells)], [VMEM] * 5, [VMEM] * 4,
    )(r_o, c_o, t_s, part, pool_part)
    edge_f, edge_t, pooled = call(
        functools.partial(edge_row_kernel, wide, narrow),
        [(chans, cells)] * 2 + [(wins, chans, cells)], [VMEM] * 4, [VMEM] * 3,
    )(m_o, t_s, edge_pre, pool_far)
    o2 = swap(pooled, "O", "near")
    e2 = swap(pooled, "E", "same")
    across = swap(pooled, "", "across")
    e_across = swap(e2, "", "across")
    o_across = swap(o2, "", "across")
    own_c, across_c = swap(pooled, "", "core"), swap(across, "", "core")
    e_c, e_across_c = swap(e2, "", "core"), swap(e_across, "", "core")
    o_c, o_across_c = swap(o2, "", "core"), swap(o_across, "", "core")
    deep_rows = wins * narrow
    sums = full(deep_rows // 2, 128, cells)
    gathered = pltpu.VMEM((deep_rows + 2, chans, cells), BF16)
    total_d, skip_f, skip_t = call(
        functools.partial(deep_near_kernel, narrow),
        [sums, volume.shape, volume.shape],
        [VMEM] * 15, [VMEM, HBM, HBM], [gathered, gathered, dma((6,))],
    )(pooled, across, own_c, across_c, e2, e_across, e_c, e_across_c, t_d, near_f, near_t, far_f, far_t, edge_f, edge_t)
    deep_shape = (1, deep_rows, 64, cells // 2)
    deep_f, deep_t = call(
        functools.partial(deep_far_kernel, wide, narrow),
        [deep_shape, deep_shape], [VMEM] * 6, [HBM] * 2,
        [gathered, pltpu.VMEM((2, deep_rows, 64, cells // 2), BF16), dma((deep_rows // 2, 2))],
    )(o2, o_across, o_c, o_across_c, t_d, total_d)
    return skip_f, skip_t, deep_f, deep_t


def solution(mesh):
    wide, narrow = mesh.shape["wide"], mesh.shape["narrow"]
    in_specs = (P("wide", "narrow", None, None), P("wide", "narrow", None, None), P(), P())
    out_specs = (
        P("wide", "narrow", None, None),
        P("wide", "narrow", None, None),
        P("wide", None, "narrow", None),
        P("wide", None, "narrow", None),
    )
    return jax.shard_map(
        functools.partial(local, wide, narrow), mesh=mesh, in_specs=in_specs, out_specs=out_specs,
        check_vma=False,
    )
```

```python
import functools

import jax
import jax.numpy as jnp
from jax import lax
from jax.experimental import pallas as pl
from jax.experimental.pallas import tpu as pltpu
from jax.sharding import PartitionSpec as P

BOTH = ("wide", "narrow")
PAD = 16
BF16 = jnp.bfloat16
F32 = jnp.float32
ANY = pl.BlockSpec(memory_space=pl.ANY)
VMEM = pl.BlockSpec(memory_space=pltpu.VMEM)
HBM = pl.BlockSpec(memory_space=pltpu.HBM)


def exchange(wide, narrow, kind, route):
    pairs = []
    for w in range(wide):
        for n in range(narrow):
            if kind == "E":
                pw = w ^ 1
            elif kind == "O":
                pw = w + 1 if w % 2 else w - 1
            else:
                pw = w
            if route == "mirror" and not 0 <= pw < wide:
                pw = w
            if not 0 <= pw < wide:
                pw, pn = w, n ^ 1
            elif route == "same" or (route == "near" and min(w, pw) != wide // 2 - 1):
                pn = n
            elif route == "core":
                pn = n ^ 1
            elif route in ("mirror", "corner") and 0 < n < narrow - 1:
                pn = narrow - 1 - n
            elif route in ("mirror", "corner"):
                if wide % 8 == 0 and (route == "corner" or (w | 4) % (wide // 2) != wide // 2 - 1):
                    pw, pn = w ^ 4, n
                else:
                    pw, pn = (w + wide // 2) % wide, narrow - 1 - n
            else:
                pn = n ^ 2
            pairs.append((w * narrow + n, pw * narrow + pn))
    return pairs


def run_copies(copies, sems):
    started = [pltpu.make_async_copy(src, dst, sems.at[k]) for k, (src, dst) in enumerate(copies)]
    for copy in started:
        copy.start()

    def wait():
        for copy in started:
            copy.wait()

    return wait


def slices_kernel(vol, tan, s_o, s_e, s_c, s_m, sems):
    w, n = lax.axis_index("wide"), lax.axis_index("narrow")
    odd = lax.rem(w, 2)
    last = vol.shape[1] - 1
    row_c = jnp.where(lax.rem(n, 2) == 0, last, 0)
    row_m = jnp.where(n < 2, last, 0)
    copies = []
    for t, src in enumerate((vol, tan)):
        for plane, face in ((odd, s_o), (1 - odd, s_e)):
            for half in range(2):
                rows = pl.ds(2 * half, 2)
                copies.append((src.at[plane, rows], face.at[t, rows]))
        copies += [(src.at[:, row_c], s_c.at[:, t]), (src.at[:, row_m], s_m.at[:, t])]
    run_copies(copies, sems)()


def weights_kernel(vol, tan, sw, dw, t_s, t_d, own, dw_half, sw_all, band, dband, sem, sems):
    n = lax.axis_index("narrow")
    wait = run_copies([(vol, own.at[0]), (tan, own.at[1])], sems)
    shallow = pltpu.make_async_copy(sw, sw_all, sem.at[0])
    deep = pltpu.make_async_copy(
        dw.at[:, :, :, :, pl.ds(pl.multiple_of((n // 2) * 128, 128), 128)], dw_half, sem.at[1]
    )
    shallow.start()
    deep.start()
    band[...] = jnp.zeros_like(band)
    dband[...] = jnp.zeros_like(dband)
    nt = (((1,), (1,)), ((), ()))

    def build(source, scratch, pick, out):
        for a in range(3):
            for c in range(3):
                for b in range(3):
                    scratch[a * 3 + c, 64 * (b + 1) : 64 * (b + 2), :] = source[a, b, c]
                for r in range(2):
                    rows = scratch[a * 3 + c, 64 * (1 - r) : 64 * (1 - r) + 256, :]
                    placed = lax.dot_general(pick, rows, nt, preferred_element_type=F32)
                    out[a, c * 128 + r * 64 : c * 128 + r * 64 + 64, :] = placed.astype(BF16)

    def selector(width, shift):
        row = lax.broadcasted_iota(jnp.int32, (64, width), 0)
        col = lax.broadcasted_iota(jnp.int32, (64, width), 1)
        return jnp.where(col == row + shift, 1.0, 0.0).astype(BF16)

    shallow.wait()
    build(sw_all, band, selector(64, 0), t_s)
    deep.wait()
    build(dw_half, dband, selector(128, 64 * lax.rem(n, 2)), t_d)
    wait()


def shifted_sum(acc, lane, first, final):
    left = pltpu.roll(acc[0:128], 1, 1)
    right = pltpu.roll(acc[256:384], acc.shape[1] - 1, 1)
    return acc[128:256] + jnp.where(first(lane), 0.0, left) + jnp.where(final(lane), 0.0, right)


def activate(pre, dot):
    s = 0.5 * jnp.tanh(0.5 * pre) + 0.5
    primal = (pre * s).astype(BF16)
    tangent = (s * (1.0 + pre * (1.0 - s)) * dot).astype(BF16)
    return primal, tangent


def pair_matrix(cells):
    source = lax.broadcasted_iota(jnp.int32, (cells, cells // 2), 0)
    target = lax.broadcasted_iota(jnp.int32, (cells, cells // 2), 1)
    return jnp.where(source // 2 == target, 0.125, 0.0).astype(BF16)


def pool_plane(out, pairing):
    halves = [jnp.dot(value, pairing, preferred_element_type=F32) for value in out]
    return jnp.concatenate(halves, axis=1)


def shallow_lanes(cells):
    lane = lax.broadcasted_iota(jnp.int32, (128, cells), 1)
    return lane, (lambda v: v == 0), (lambda v: v == cells - 1)


def row_windows(face, core_row, far_row, n, narrow):
    rows, chans, cells = face.shape
    far_row = jnp.where((n > 0) & (n < narrow - 1), far_row, jnp.zeros_like(far_row))
    even = lax.rem(n, 2) == 0
    top, bottom = jnp.where(even, far_row, core_row), jnp.where(even, core_row, far_row)
    flat = face.reshape(rows * chans, cells)
    return (
        jnp.concatenate([top, flat[: 3 * chans]], axis=0),
        jnp.concatenate([flat[chans:], bottom], axis=0),
    )


def edge_kernel(face, *rest):
    row_c, row_m = rest[-2:]
    n = lax.axis_index("narrow")
    last = face.shape[1] - 1
    for t in range(2):
        for row, is_last in ((row_c, lax.rem(n, 2) == 0), (row_m, n < 2)):
            chans = face.shape[2]
            row[t, 0:chans] = jnp.where(is_last, face[t, last], face[t, 0])
            if row.shape[1] > chans:
                row[t, chans:] = jnp.zeros((row.shape[1] - chans, face.shape[3]), BF16)


def own_kernel(narrow, x, r_c, r_m, t_s, part):
    n = lax.axis_index("narrow")
    cells = x.shape[4]
    lane, first, final = shallow_lanes(cells)
    for t in range(2):
        stacks = [row_windows(x[t, p], r_c[p, t], r_m[p, t], n, narrow) for p in range(2)]
        for win in range(2):
            stack = jnp.concatenate([stacks[0][win], stacks[1][win]], axis=0)
            for q in range(2):
                taps = jnp.concatenate([t_s[1 - q], t_s[2 - q]], axis=1)
                acc = jnp.dot(taps, stack, preferred_element_type=F32)
                part[q, t, win] = shifted_sum(acc, lane, first, final)


def finish_plane(narrow, q, taps, face, core_row, far_row, part, emit):
    n = lax.axis_index("narrow")
    chans, cells = face.shape[2:]
    lane, first, final = shallow_lanes(cells)
    pairing = pair_matrix(cells)
    stacks = []
    for t in range(2):
        far = jnp.zeros((chans, cells), BF16) if far_row is None else far_row[t, 0:chans]
        stacks.append(row_windows(face[t], core_row[t, 0:chans], far, n, narrow))
    for win in range(2):
        pre = []
        for t in range(2):
            acc = jnp.dot(taps, stacks[t][win], preferred_element_type=F32)
            pre.append(part[q, t, win] + shifted_sum(acc, lane, first, final))
        out = activate(*pre)
        emit(win, pre, [v.reshape(2, 64, cells) for v in out], pool_plane(out, pairing))


def near_kernel(narrow, r_e, c_e, m_e, t_s, part, skip_f, skip_t, pool_part):
    odd = lax.rem(lax.axis_index("wide"), 2)

    def emit(win, pre, out, pool):
        for t, ref in enumerate((skip_f, skip_t)):
            ref[2 * win : 2 * win + 2] = out[t]
        pool_part[win] = pool[0:64] + pool[64:128]

    finish_plane(narrow, 1 - odd, t_s[2 - 2 * odd], r_e, c_e, m_e, part, emit)


def far_taps(wide, t_s):
    w = lax.axis_index("wide")
    taps = t_s[2 * lax.rem(w, 2)]
    return jnp.where((w > 0) & (w < wide - 1), taps, jnp.zeros_like(taps))


def far_kernel(wide, narrow, r_o, c_o, t_s, part, pool_part, skip_f, skip_t, pool_far, edge_pre):
    odd = lax.rem(lax.axis_index("wide"), 2)
    even_n = lax.rem(lax.axis_index("narrow"), 2) == 0

    def emit(win, pre, out, pool):
        for t, ref in enumerate((skip_f, skip_t)):
            ref[2 * win : 2 * win + 2] = out[t]
        none = jnp.zeros_like(pool[0:64])
        if win == 0:
            pool_far[0] = pool_part[0] + jnp.where(even_n, none, pool[0:64]) + pool[64:128]
            for t in range(2):
                edge_pre[t] = pre[t][0:64]
        else:
            pool_far[1] = pool_part[1] + pool[0:64] + jnp.where(even_n, pool[64:128], none)
            for t in range(2):
                edge_pre[t] = jnp.where(even_n, edge_pre[t], pre[t][64:128])

    finish_plane(narrow, odd, far_taps(wide, t_s), r_o, c_o, None, part, emit)


def edge_row_kernel(wide, narrow, m_o, t_s, edge_pre, pool_far, edge_f, edge_t, pooled):
    n = lax.axis_index("narrow")
    chans, cells = edge_pre.shape[1:]
    even_n = lax.rem(n, 2) == 0
    has_m = (n > 0) & (n < narrow - 1)
    lane, first, final = shallow_lanes(cells)
    taps = far_taps(wide, t_s)
    pre = []
    for t in range(2):
        row = m_o[t, 0:chans]
        row = jnp.where(has_m, row, jnp.zeros_like(row))
        none = jnp.zeros_like(row)
        stack = [jnp.where(even_n, row, none), none, none, jnp.where(even_n, none, row)]
        acc = jnp.dot(taps, jnp.concatenate(stack, axis=0), preferred_element_type=F32)
        both = shifted_sum(acc, lane, first, final)
        pre.append(edge_pre[t] + jnp.where(even_n, both[0:chans], both[chans:]))
    out = activate(*pre)
    edge_f[...], edge_t[...] = out
    pool = pool_plane(out, pair_matrix(cells))
    for win in range(2):
        mine = even_n if win == 0 else jnp.logical_not(even_n)
        pooled[win] = (pool_far[win] + jnp.where(mine, pool, jnp.zeros_like(pool))).astype(BF16)


def deep_lanes(cells):
    lane = lax.broadcasted_iota(jnp.int32, (128, 2 * cells), 1)
    first = lambda v: (v == 0) | (v == cells)
    final = lambda v: (v == cells - 1) | (v == 2 * cells - 1)
    return lane, first, final


def gather_rows(x, parts, far, narrow):
    n = lax.axis_index("narrow")
    sib = n + 1 - 2 * lax.rem(n, 2)
    pair = parts[0].shape[0]
    x[0] = jnp.zeros(x.shape[1:], BF16)
    x[narrow * pair + 1] = jnp.zeros(x.shape[1:], BF16)
    for k, source in enumerate(parts):
        member = n if k < 2 else sib
        owner = lax.rem(member + 2 * (k % 2), narrow)
        if far is not None:
            owner = jnp.where(far, lax.rem(member + 2 - 2 * (k % 2), narrow), owner)
        x[pl.ds(owner * pair + 1, pair)] = source[...]


def deep_sum(x, taps, j, lane, first, final):
    stack = x[2 * j : 2 * j + 4].reshape(256, x.shape[2])
    acc = jnp.dot(taps, stack, preferred_element_type=F32)
    return shifted_sum(acc, lane, first, final)


def copy_planes(near_f, near_t, far_f, far_t, edge_f, edge_t, skip_f, skip_t, sems):
    odd = lax.rem(lax.axis_index("wide"), 2)
    even_n = lax.rem(lax.axis_index("narrow"), 2) == 0
    last = far_f.shape[0] - 1
    edge, rest = jnp.where(even_n, 0, last), pl.ds(jnp.where(even_n, 1, 0), last)
    copies = []
    for near, far, row, skip in ((near_f, far_f, edge_f, skip_f), (near_t, far_t, edge_t, skip_t)):
        copies += [
            (near, skip.at[1 - odd]),
            (far.at[rest], skip.at[odd, rest]),
            (row, skip.at[odd, edge]),
        ]
    return run_copies(copies, sems)


def deep_near_kernel(narrow, own, across, own_c, across_c, e, e_across, e_c, e_across_c, t_d, total, x, y):
    odd = lax.rem(lax.axis_index("wide"), 2)
    gather_rows(x, (own, across, own_c, across_c), None, narrow)
    gather_rows(y, (e, e_across, e_c, e_across_c), None, narrow)
    cells = x.shape[2]
    lanes = deep_lanes(cells // 2)
    taps = jnp.concatenate([t_d[1], t_d[2 - 2 * odd]], axis=1)
    for j in range(total.shape[0]):
        stack = [v[2 * j : 2 * j + 4].reshape(256, cells) for v in (x, y)]
        acc = jnp.dot(taps, jnp.concatenate(stack, axis=0), preferred_element_type=F32)
        total[j] = shifted_sum(acc, *lanes)


def deep_far_kernel(wide, narrow, o, o_across, o_c, o_across_c, t_d, part, near_f, near_t,
                    far_f, far_t, edge_f, edge_t, out_f, out_t, skip_f, skip_t, x, staged, sems, skip_sems):
    planes = (near_f, near_t, far_f, far_t, edge_f, edge_t, skip_f, skip_t)
    waits = [copy_planes(*planes, skip_sems)]
    w = lax.axis_index("wide")
    cells = x.shape[2] // 2
    far = (w == wide // 2 - 1) | (w == wide // 2)
    gather_rows(x, (o, o_across, o_c, o_across_c), far, narrow)
    lanes = deep_lanes(cells)
    taps = far_taps(wide, t_d)
    for j in range(part.shape[0]):
        both = part[j] + deep_sum(x, taps, j, *lanes)
        out = activate(both[:, :cells], both[:, cells:])
        rows = pl.ds(2 * j, 2)
        copies = []
        for t, ref in enumerate((out_f, out_t)):
            staged[t, 2 * j : 2 * j + 2] = out[t].reshape(2, 64, cells)
            copies.append((staged.at[t, rows], ref.at[0, rows]))
        waits.append(run_copies(copies, sems.at[j]))
    for wait in waits:
        wait()


def call(body, outs, in_specs, out_specs, scratch=()):
    return pl.pallas_call(
        body,
        out_shape=[o if hasattr(o, "dtype") else jax.ShapeDtypeStruct(o, BF16) for o in outs],
        in_specs=in_specs,
        out_specs=out_specs,
        scratch_shapes=list(scratch),
        compiler_params=pltpu.CompilerParams(vmem_limit_bytes=32 * 1024 * 1024),
        cost_estimate=pl.CostEstimate(flops=0, bytes_accessed=0, transcendentals=0),
    )


def local(wide, narrow, volume, volume_tangent, shallow_weight, deep_weight):
    planes, rows, chans, cells = volume.shape
    volume, volume_tangent, shallow_weight, deep_weight = (
        pltpu.with_memory_space_constraint(v, pltpu.HBM)
        for v in (volume, volume_tangent, shallow_weight, deep_weight)
    )
    dma = pltpu.SemaphoreType.DMA

    def swap(v, kind, route):
        return lax.ppermute(v, BOTH, exchange(wide, narrow, kind, route))

    def full(*shape):
        return jax.ShapeDtypeStruct(shape, F32)

    plane, edge = (rows, chans, cells), (planes, 2, chans, cells)
    s_o, s_e, s_c, s_m = call(
        slices_kernel, [(2,) + plane, (2,) + plane, edge, edge],
        [HBM] * 2, [ANY] * 4, [dma((12,))],
    )(volume, volume_tangent)
    r_o = swap(s_o, "O", "same")
    r_e = swap(s_e, "E", "same")
    r_c = swap(s_c, "", "core")
    r_m = swap(s_m, "", "mirror")
    band = (3, 384, 256)
    t_s, t_d, own = call(
        weights_kernel, [band, band, (2,) + volume.shape], [HBM] * 4, [VMEM, VMEM, ANY],
        [
            pltpu.VMEM((3, 3, 3, 64, 128), BF16),
            pltpu.VMEM((3, 3, 3, 64, 64), BF16),
            pltpu.VMEM((9, 320, 64), BF16),
            pltpu.VMEM((9, 320, 128), BF16),
            dma((2,)),
            dma((2,)),
        ],
    )(volume, volume_tangent, shallow_weight, deep_weight)
    wins = rows // 2
    (part,) = call(
        functools.partial(own_kernel, narrow),
        [full(planes, 2, wins, 128, cells)], [VMEM] * 4, [VMEM],
    )(own, r_c, r_m, t_s)
    row_ec, row_em = call(edge_kernel, [(2, chans + 2 * PAD, cells)] * 2, [VMEM], [VMEM] * 2)(r_e)
    c_e, m_e = swap(row_ec, "", "core"), swap(row_em, "", "corner")
    row_oc, row_om = call(edge_kernel, [(2, chans, cells), (2, chans + PAD, cells)], [VMEM] * 3, [VMEM] * 2)(r_o, part, row_ec)
    c_o, m_o = swap(row_oc, "", "core"), swap(row_om, "", "corner")
    near_f, near_t, pool_part = call(
        functools.partial(near_kernel, narrow),
        [plane, plane, full(wins, chans, cells)], [VMEM] * 5, [VMEM] * 3,
    )(r_e, c_e, m_e, t_s, part)
    far_f, far_t, pool_far, edge_pre = call(
        functools.partial(far_kernel, wide, narrow),
        [plane, plane, full(wins, chans, cells), full(2, chans, cells)], [VMEM] * 5, [VMEM] * 4,
    )(r_o, c_o, t_s, part, pool_part)
    edge_f, edge_t, pooled = call(
        functools.partial(edge_row_kernel, wide, narrow),
        [(chans, cells)] * 2 + [(wins, chans, cells)], [VMEM] * 4, [VMEM] * 3,
    )(m_o, t_s, edge_pre, pool_far)
    o2 = swap(pooled, "O", "near")
    e2 = swap(pooled, "E", "same")
    across = swap(pooled, "", "across")
    e_across = swap(e2, "", "across")
    o_across = swap(o2, "", "across")
    own_c, across_c = swap(pooled, "", "core"), swap(across, "", "core")
    e_c, e_across_c = swap(e2, "", "core"), swap(e_across, "", "core")
    o_c, o_across_c = swap(o2, "", "core"), swap(o_across, "", "core")
    deep_rows = wins * narrow
    sums = full(deep_rows // 2, 128, cells)
    gathered = pltpu.VMEM((deep_rows + 2, chans, cells), BF16)
    (total_d,) = call(
        functools.partial(deep_near_kernel, narrow),
        [sums], [VMEM] * 9, [VMEM], [gathered, gathered],
    )(pooled, across, own_c, across_c, e2, e_across, e_c, e_across_c, t_d)
    deep_shape = (1, deep_rows, 64, cells // 2)
    staged = pltpu.VMEM((2, deep_rows, 64, cells // 2), BF16)
    deep_f, deep_t, skip_f, skip_t = call(
        functools.partial(deep_far_kernel, wide, narrow),
        [deep_shape, deep_shape, volume.shape, volume.shape], [VMEM] * 12, [HBM] * 4,
        [gathered, staged, dma((deep_rows // 2, 2)), dma((6,))],
    )(o2, o_across, o_c, o_across_c, t_d, total_d, near_f, near_t, far_f, far_t, edge_f, edge_t)
    return skip_f, skip_t, deep_f, deep_t


def solution(mesh):
    wide, narrow = mesh.shape["wide"], mesh.shape["narrow"]
    in_specs = (P("wide", "narrow", None, None), P("wide", "narrow", None, None), P(), P())
    out_specs = (
        P("wide", "narrow", None, None),
        P("wide", "narrow", None, None),
        P("wide", None, "narrow", None),
        P("wide", None, "narrow", None),
    )
    return jax.shard_map(
        functools.partial(local, wide, narrow), mesh=mesh, in_specs=in_specs, out_specs=out_specs,
        check_vma=False,
    )
```

```python
import functools

import jax
import jax.numpy as jnp
from jax import lax
from jax.experimental import pallas as pl
from jax.experimental.pallas import tpu as pltpu
from jax.sharding import PartitionSpec as P

BOTH = ("wide", "narrow")
PAD = 16
BF16 = jnp.bfloat16
F32 = jnp.float32
ANY = pl.BlockSpec(memory_space=pl.ANY)
VMEM = pl.BlockSpec(memory_space=pltpu.VMEM)
HBM = pl.BlockSpec(memory_space=pltpu.HBM)


def exchange(wide, narrow, kind, route):
    pairs = []
    for w in range(wide):
        for n in range(narrow):
            if kind == "E":
                pw = w ^ 1
            elif kind == "O":
                pw = w + 1 if w % 2 else w - 1
            else:
                pw = w
            if route == "mirror" and not 0 <= pw < wide:
                pw = w
            if not 0 <= pw < wide:
                pw, pn = w, n ^ 1
            elif route == "same" or (route == "near" and min(w, pw) != wide // 2 - 1):
                pn = n
            elif route == "core":
                pn = n ^ 1
            elif route in ("mirror", "corner") and 0 < n < narrow - 1:
                pn = narrow - 1 - n
            elif route in ("mirror", "corner"):
                if wide % 8 == 0 and (route == "corner" or (w | 4) % (wide // 2) != wide // 2 - 1):
                    pw, pn = w ^ 4, n
                else:
                    pw, pn = (w + wide // 2) % wide, narrow - 1 - n
            else:
                pn = n ^ 2
            pairs.append((w * narrow + n, pw * narrow + pn))
    return pairs


def run_copies(copies, sems):
    started = [pltpu.make_async_copy(src, dst, sems.at[k]) for k, (src, dst) in enumerate(copies)]
    for copy in started:
        copy.start()

    def wait():
        for copy in started:
            copy.wait()

    return wait


def slices_kernel(vol, tan, s_o, s_e, s_c, s_m, sems):
    w, n = lax.axis_index("wide"), lax.axis_index("narrow")
    odd = lax.rem(w, 2)
    last = vol.shape[1] - 1
    row_c = jnp.where(lax.rem(n, 2) == 0, last, 0)
    row_m = jnp.where(n < 2, last, 0)
    copies = []
    for t, src in enumerate((vol, tan)):
        for plane, face in ((odd, s_o), (1 - odd, s_e)):
            for half in range(2):
                rows = pl.ds(2 * half, 2)
                copies.append((src.at[plane, rows], face.at[t, rows]))
        copies += [(src.at[:, row_c], s_c.at[:, t]), (src.at[:, row_m], s_m.at[:, t])]
    run_copies(copies, sems)()


def weights_kernel(vol, tan, sw, dw, t_s, t_d, own, dw_half, sw_all, band, dband, sem, sems):
    n = lax.axis_index("narrow")
    wait = run_copies([(vol, own.at[0]), (tan, own.at[1])], sems)
    shallow = pltpu.make_async_copy(sw, sw_all, sem.at[0])
    deep = pltpu.make_async_copy(
        dw.at[:, :, :, :, pl.ds(pl.multiple_of((n // 2) * 128, 128), 128)], dw_half, sem.at[1]
    )
    shallow.start()
    deep.start()
    band[...] = jnp.zeros_like(band)
    dband[...] = jnp.zeros_like(dband)
    nt = (((1,), (1,)), ((), ()))

    def build(source, scratch, pick, out):
        for a in range(3):
            for c in range(3):
                for b in range(3):
                    scratch[a * 3 + c, 64 * (b + 1) : 64 * (b + 2), :] = source[a, b, c]
                for r in range(2):
                    rows = scratch[a * 3 + c, 64 * (1 - r) : 64 * (1 - r) + 256, :]
                    placed = lax.dot_general(pick, rows, nt, preferred_element_type=F32)
                    out[a, c * 128 + r * 64 : c * 128 + r * 64 + 64, :] = placed.astype(BF16)

    def selector(width, shift):
        row = lax.broadcasted_iota(jnp.int32, (64, width), 0)
        col = lax.broadcasted_iota(jnp.int32, (64, width), 1)
        return jnp.where(col == row + shift, 1.0, 0.0).astype(BF16)

    shallow.wait()
    build(sw_all, band, selector(64, 0), t_s)
    deep.wait()
    build(dw_half, dband, selector(128, 64 * lax.rem(n, 2)), t_d)
    wait()


def shifted_sum(acc, lane, first, final):
    rows = acc.shape[0] // 3
    left = pltpu.roll(acc[0:rows], 1, 1)
    right = pltpu.roll(acc[2 * rows :], acc.shape[1] - 1, 1)
    return acc[rows : 2 * rows] + jnp.where(first(lane), 0.0, left) + jnp.where(final(lane), 0.0, right)


def activate(pre, dot):
    s = 0.5 * jnp.tanh(0.5 * pre) + 0.5
    primal = (pre * s).astype(BF16)
    tangent = (s * (1.0 + pre * (1.0 - s)) * dot).astype(BF16)
    return primal, tangent


def pair_matrix(cells):
    source = lax.broadcasted_iota(jnp.int32, (cells, cells // 2), 0)
    target = lax.broadcasted_iota(jnp.int32, (cells, cells // 2), 1)
    return jnp.where(source // 2 == target, 0.125, 0.0).astype(BF16)


def pool_plane(out, pairing):
    halves = [jnp.dot(value, pairing, preferred_element_type=F32) for value in out]
    return jnp.concatenate(halves, axis=1)


def shallow_lanes(cells):
    lane = lax.broadcasted_iota(jnp.int32, (128, cells), 1)
    return lane, (lambda v: v == 0), (lambda v: v == cells - 1)


def row_windows(face, core_row, far_row, n, narrow):
    rows, chans, cells = face.shape
    far_row = jnp.where((n > 0) & (n < narrow - 1), far_row, jnp.zeros_like(far_row))
    even = lax.rem(n, 2) == 0
    top, bottom = jnp.where(even, far_row, core_row), jnp.where(even, core_row, far_row)
    flat = face.reshape(rows * chans, cells)
    return (
        jnp.concatenate([top, flat[: 3 * chans]], axis=0),
        jnp.concatenate([flat[chans:], bottom], axis=0),
    )


def edge_kernel(face, *rest):
    row_c, row_m = rest[-2:]
    n = lax.axis_index("narrow")
    last = face.shape[1] - 1
    for t in range(2):
        for row, is_last in ((row_c, lax.rem(n, 2) == 0), (row_m, n < 2)):
            chans = face.shape[2]
            row[t, 0:chans] = jnp.where(is_last, face[t, last], face[t, 0])
            if row.shape[1] > chans:
                row[t, chans:] = jnp.zeros((row.shape[1] - chans, face.shape[3]), BF16)


def own_kernel(narrow, x, r_c, r_m, t_s, part):
    n = lax.axis_index("narrow")
    cells = x.shape[4]
    lane, first, final = shallow_lanes(cells)
    for t in range(2):
        stacks = [row_windows(x[t, p], r_c[p, t], r_m[p, t], n, narrow) for p in range(2)]
        for win in range(2):
            stack = jnp.concatenate([stacks[0][win], stacks[1][win]], axis=0)
            for q in range(2):
                taps = jnp.concatenate([t_s[1 - q], t_s[2 - q]], axis=1)
                acc = jnp.dot(taps, stack, preferred_element_type=F32)
                part[q, t, win] = shifted_sum(acc, lane, first, final)


def finish_plane(narrow, q, taps, face, core_row, far_row, part, emit):
    n = lax.axis_index("narrow")
    chans, cells = face.shape[2:]
    lane, first, final = shallow_lanes(cells)
    pairing = pair_matrix(cells)
    stacks = []
    for t in range(2):
        far = jnp.zeros((chans, cells), BF16) if far_row is None else far_row[t, 0:chans]
        stacks.append(row_windows(face[t], core_row[t, 0:chans], far, n, narrow))
    for win in range(2):
        pre = []
        for t in range(2):
            acc = jnp.dot(taps, stacks[t][win], preferred_element_type=F32)
            pre.append(part[q, t, win] + shifted_sum(acc, lane, first, final))
        out = activate(*pre)
        emit(win, pre, [v.reshape(2, 64, cells) for v in out], pool_plane(out, pairing))


def near_kernel(narrow, r_e, c_e, m_e, t_s, part, skip_f, skip_t, pool_part):
    odd = lax.rem(lax.axis_index("wide"), 2)

    def emit(win, pre, out, pool):
        for t, ref in enumerate((skip_f, skip_t)):
            ref[2 * win : 2 * win + 2] = out[t]
        pool_part[win] = pool[0:64] + pool[64:128]

    finish_plane(narrow, 1 - odd, t_s[2 - 2 * odd], r_e, c_e, m_e, part, emit)


def far_taps(wide, t_s):
    w = lax.axis_index("wide")
    taps = t_s[2 * lax.rem(w, 2)]
    return jnp.where((w > 0) & (w < wide - 1), taps, jnp.zeros_like(taps))


def far_kernel(wide, narrow, r_o, c_o, t_s, part, pool_part, skip_f, skip_t, pool_far, edge_pre):
    odd = lax.rem(lax.axis_index("wide"), 2)
    even_n = lax.rem(lax.axis_index("narrow"), 2) == 0

    def emit(win, pre, out, pool):
        for t, ref in enumerate((skip_f, skip_t)):
            ref[2 * win : 2 * win + 2] = out[t]
        none = jnp.zeros_like(pool[0:64])
        if win == 0:
            pool_far[0] = pool_part[0] + jnp.where(even_n, none, pool[0:64]) + pool[64:128]
            for t in range(2):
                edge_pre[t] = pre[t][0:64]
        else:
            pool_far[1] = pool_part[1] + pool[0:64] + jnp.where(even_n, pool[64:128], none)
            for t in range(2):
                edge_pre[t] = jnp.where(even_n, edge_pre[t], pre[t][64:128])

    finish_plane(narrow, odd, far_taps(wide, t_s), r_o, c_o, None, part, emit)


def edge_row_kernel(wide, narrow, m_o, t_s, edge_pre, pool_far, edge_f, edge_t, pooled):
    n = lax.axis_index("narrow")
    chans, cells = edge_pre.shape[1:]
    even_n = lax.rem(n, 2) == 0
    has_m = (n > 0) & (n < narrow - 1)
    lane, first, final = shallow_lanes(cells)
    taps = far_taps(wide, t_s)
    upper = jnp.concatenate([taps[2 * c * chans : (2 * c + 1) * chans] for c in range(3)], axis=0)
    lower = jnp.concatenate([taps[(2 * c + 1) * chans : (2 * c + 2) * chans] for c in range(3)], axis=0)
    taps = jnp.where(even_n, upper, lower)
    pre = []
    for t in range(2):
        row = m_o[t, 0:chans]
        row = jnp.where(has_m, row, jnp.zeros_like(row))
        none = jnp.zeros_like(row)
        stack = [jnp.where(even_n, row, none), none, none, jnp.where(even_n, none, row)]
        acc = jnp.dot(taps, jnp.concatenate(stack, axis=0), preferred_element_type=F32)
        pre.append(edge_pre[t] + shifted_sum(acc, lane[0:chans], first, final))
    out = activate(*pre)
    edge_f[...], edge_t[...] = out
    pool = pool_plane(out, pair_matrix(cells))
    for win in range(2):
        mine = even_n if win == 0 else jnp.logical_not(even_n)
        pooled[win] = (pool_far[win] + jnp.where(mine, pool, jnp.zeros_like(pool))).astype(BF16)


def deep_lanes(cells):
    lane = lax.broadcasted_iota(jnp.int32, (128, 2 * cells), 1)
    first = lambda v: (v == 0) | (v == cells)
    final = lambda v: (v == cells - 1) | (v == 2 * cells - 1)
    return lane, first, final


def gather_rows(x, parts, far, narrow):
    n = lax.axis_index("narrow")
    sib = n + 1 - 2 * lax.rem(n, 2)
    pair = parts[0].shape[0]
    x[0] = jnp.zeros(x.shape[1:], BF16)
    x[narrow * pair + 1] = jnp.zeros(x.shape[1:], BF16)
    for k, source in enumerate(parts):
        member = n if k < 2 else sib
        owner = lax.rem(member + 2 * (k % 2), narrow)
        if far is not None:
            owner = jnp.where(far, lax.rem(member + 2 - 2 * (k % 2), narrow), owner)
        x[pl.ds(owner * pair + 1, pair)] = source[...]


def deep_sum(x, taps, j, lane, first, final):
    stack = x[2 * j : 2 * j + 4].reshape(256, x.shape[2])
    acc = jnp.dot(taps, stack, preferred_element_type=F32)
    return shifted_sum(acc, lane, first, final)


def copy_planes(near_f, near_t, far_f, far_t, edge_f, edge_t, skip_f, skip_t, sems):
    odd = lax.rem(lax.axis_index("wide"), 2)
    even_n = lax.rem(lax.axis_index("narrow"), 2) == 0
    last = far_f.shape[0] - 1
    edge, rest = jnp.where(even_n, 0, last), pl.ds(jnp.where(even_n, 1, 0), last)
    copies = []
    for near, far, row, skip in ((near_f, far_f, edge_f, skip_f), (near_t, far_t, edge_t, skip_t)):
        copies += [
            (near, skip.at[1 - odd]),
            (far.at[rest], skip.at[odd, rest]),
            (row, skip.at[odd, edge]),
        ]
    return run_copies(copies, sems)


def deep_near_kernel(narrow, own, across, own_c, across_c, e, e_across, e_c, e_across_c, t_d, total, x, y):
    odd = lax.rem(lax.axis_index("wide"), 2)
    gather_rows(x, (own, across, own_c, across_c), None, narrow)
    gather_rows(y, (e, e_across, e_c, e_across_c), None, narrow)
    cells = x.shape[2]
    lanes = deep_lanes(cells // 2)
    taps = jnp.concatenate([t_d[1], t_d[2 - 2 * odd]], axis=1)
    for j in range(total.shape[0]):
        stack = [v[2 * j : 2 * j + 4].reshape(256, cells) for v in (x, y)]
        acc = jnp.dot(taps, jnp.concatenate(stack, axis=0), preferred_element_type=F32)
        total[j] = shifted_sum(acc, *lanes)


def deep_far_kernel(wide, narrow, o, o_across, o_c, o_across_c, t_d, part, near_f, near_t,
                    far_f, far_t, edge_f, edge_t, out_f, out_t, skip_f, skip_t, x, staged, sems, skip_sems):
    planes = (near_f, near_t, far_f, far_t, edge_f, edge_t, skip_f, skip_t)
    waits = [copy_planes(*planes, skip_sems)]
    w = lax.axis_index("wide")
    cells = x.shape[2] // 2
    far = (w == wide // 2 - 1) | (w == wide // 2)
    gather_rows(x, (o, o_across, o_c, o_across_c), far, narrow)
    lanes = deep_lanes(cells)
    taps = far_taps(wide, t_d)
    for j in range(part.shape[0]):
        both = part[j] + deep_sum(x, taps, j, *lanes)
        out = activate(both[:, :cells], both[:, cells:])
        rows = pl.ds(2 * j, 2)
        copies = []
        for t, ref in enumerate((out_f, out_t)):
            staged[t, 2 * j : 2 * j + 2] = out[t].reshape(2, 64, cells)
            copies.append((staged.at[t, rows], ref.at[0, rows]))
        waits.append(run_copies(copies, sems.at[j]))
    for wait in waits:
        wait()


def call(body, outs, in_specs, out_specs, scratch=()):
    return pl.pallas_call(
        body,
        out_shape=[o if hasattr(o, "dtype") else jax.ShapeDtypeStruct(o, BF16) for o in outs],
        in_specs=in_specs,
        out_specs=out_specs,
        scratch_shapes=list(scratch),
        compiler_params=pltpu.CompilerParams(vmem_limit_bytes=32 * 1024 * 1024),
        cost_estimate=pl.CostEstimate(flops=0, bytes_accessed=0, transcendentals=0),
    )


def local(wide, narrow, volume, volume_tangent, shallow_weight, deep_weight):
    planes, rows, chans, cells = volume.shape
    volume, volume_tangent, shallow_weight, deep_weight = (
        pltpu.with_memory_space_constraint(v, pltpu.HBM)
        for v in (volume, volume_tangent, shallow_weight, deep_weight)
    )
    dma = pltpu.SemaphoreType.DMA

    def swap(v, kind, route):
        return lax.ppermute(v, BOTH, exchange(wide, narrow, kind, route))

    def full(*shape):
        return jax.ShapeDtypeStruct(shape, F32)

    plane, edge = (rows, chans, cells), (planes, 2, chans, cells)
    s_o, s_e, s_c, s_m = call(
        slices_kernel, [(2,) + plane, (2,) + plane, edge, edge],
        [HBM] * 2, [ANY] * 4, [dma((12,))],
    )(volume, volume_tangent)
    r_o = swap(s_o, "O", "same")
    r_e = swap(s_e, "E", "same")
    r_c = swap(s_c, "", "core")
    r_m = swap(s_m, "", "mirror")
    band = (3, 384, 256)
    t_s, t_d, own = call(
        weights_kernel, [band, band, (2,) + volume.shape], [HBM] * 4, [VMEM, VMEM, ANY],
        [
            pltpu.VMEM((3, 3, 3, 64, 128), BF16),
            pltpu.VMEM((3, 3, 3, 64, 64), BF16),
            pltpu.VMEM((9, 320, 64), BF16),
            pltpu.VMEM((9, 320, 128), BF16),
            dma((2,)),
            dma((2,)),
        ],
    )(volume, volume_tangent, shallow_weight, deep_weight)
    wins = rows // 2
    (part,) = call(
        functools.partial(own_kernel, narrow),
        [full(planes, 2, wins, 128, cells)], [VMEM] * 4, [VMEM],
    )(own, r_c, r_m, t_s)
    row_ec, row_em = call(edge_kernel, [(2, chans + 2 * PAD, cells)] * 2, [VMEM], [VMEM] * 2)(r_e)
    c_e, m_e = swap(row_ec, "", "core"), swap(row_em, "", "corner")
    row_oc, row_om = call(edge_kernel, [(2, chans, cells)] * 2, [VMEM] * 3, [VMEM] * 2)(r_o, part, row_ec)
    m_o = swap(row_om, "", "corner")
    c_o = swap(row_oc, "", "core")
    near_f, near_t, pool_part = call(
        functools.partial(near_kernel, narrow),
        [plane, plane, full(wins, chans, cells)], [VMEM] * 5, [VMEM] * 3,
    )(r_e, c_e, m_e, t_s, part)
    far_f, far_t, pool_far, edge_pre = call(
        functools.partial(far_kernel, wide, narrow),
        [plane, plane, full(wins, chans, cells), full(2, chans, cells)], [VMEM] * 5, [VMEM] * 4,
    )(r_o, c_o, t_s, part, pool_part)
    edge_f, edge_t, pooled = call(
        functools.partial(edge_row_kernel, wide, narrow),
        [(chans, cells)] * 2 + [(wins, chans, cells)], [VMEM] * 4, [VMEM] * 3,
    )(m_o, t_s, edge_pre, pool_far)
    o2 = swap(pooled, "O", "near")
    e2 = swap(pooled, "E", "same")
    across = swap(pooled, "", "across")
    e_across = swap(e2, "", "across")
    o_across = swap(o2, "", "across")
    own_c, across_c = swap(pooled, "", "core"), swap(across, "", "core")
    e_c, e_across_c = swap(e2, "", "core"), swap(e_across, "", "core")
    o_c, o_across_c = swap(o2, "", "core"), swap(o_across, "", "core")
    deep_rows = wins * narrow
    sums = full(deep_rows // 2, 128, cells)
    gathered = pltpu.VMEM((deep_rows + 2, chans, cells), BF16)
    (total_d,) = call(
        functools.partial(deep_near_kernel, narrow),
        [sums], [VMEM] * 9, [VMEM], [gathered, gathered],
    )(pooled, across, own_c, across_c, e2, e_across, e_c, e_across_c, t_d)
    deep_shape = (1, deep_rows, 64, cells // 2)
    staged = pltpu.VMEM((2, deep_rows, 64, cells // 2), BF16)
    deep_f, deep_t, skip_f, skip_t = call(
        functools.partial(deep_far_kernel, wide, narrow),
        [deep_shape, deep_shape, volume.shape, volume.shape], [VMEM] * 12, [HBM] * 4,
        [gathered, staged, dma((deep_rows // 2, 2)), dma((6,))],
    )(o2, o_across, o_c, o_across_c, t_d, total_d, near_f, near_t, far_f, far_t, edge_f, edge_t)
    return skip_f, skip_t, deep_f, deep_t


def solution(mesh):
    wide, narrow = mesh.shape["wide"], mesh.shape["narrow"]
    in_specs = (P("wide", "narrow", None, None), P("wide", "narrow", None, None), P(), P())
    out_specs = (
        P("wide", "narrow", None, None),
        P("wide", "narrow", None, None),
        P("wide", None, "narrow", None),
        P("wide", None, "narrow", None),
    )
    return jax.shard_map(
        functools.partial(local, wide, narrow), mesh=mesh, in_specs=in_specs, out_specs=out_specs,
        check_vma=False,
    )
```

```python
import functools

import jax
import jax.numpy as jnp
from jax import lax
from jax.experimental import pallas as pl
from jax.experimental.pallas import tpu as pltpu
from jax.sharding import PartitionSpec as P

BOTH = ("wide", "narrow")
PAD = 16
BF16 = jnp.bfloat16
F32 = jnp.float32
ANY = pl.BlockSpec(memory_space=pl.ANY)
VMEM = pl.BlockSpec(memory_space=pltpu.VMEM)
HBM = pl.BlockSpec(memory_space=pltpu.HBM)


def exchange(wide, narrow, kind, route):
    pairs = []
    for w in range(wide):
        for n in range(narrow):
            if kind == "E":
                pw = w ^ 1
            elif kind == "O":
                pw = w + 1 if w % 2 else w - 1
            else:
                pw = w
            if route == "mirror" and not 0 <= pw < wide:
                pw = w
            if not 0 <= pw < wide:
                pw, pn = w, n ^ 1
            elif route == "same" or (route == "near" and min(w, pw) != wide // 2 - 1):
                pn = n
            elif route == "core":
                pn = n ^ 1
            elif route in ("mirror", "corner") and 0 < n < narrow - 1:
                pn = narrow - 1 - n
            elif route in ("mirror", "corner"):
                if wide % 8 == 0 and (route == "corner" or (w | 4) % (wide // 2) != wide // 2 - 1):
                    pw, pn = w ^ 4, n
                else:
                    pw, pn = (w + wide // 2) % wide, narrow - 1 - n
            else:
                pn = n ^ 2
            pairs.append((w * narrow + n, pw * narrow + pn))
    return pairs


def run_copies(copies, sems):
    started = [pltpu.make_async_copy(src, dst, sems.at[k]) for k, (src, dst) in enumerate(copies)]
    for copy in started:
        copy.start()

    def wait():
        for copy in started:
            copy.wait()

    return wait


def slices_kernel(vol, tan, s_o, s_e, s_c, s_m, sems):
    w, n = lax.axis_index("wide"), lax.axis_index("narrow")
    odd = lax.rem(w, 2)
    last = vol.shape[1] - 1
    row_c = jnp.where(lax.rem(n, 2) == 0, last, 0)
    row_m = jnp.where(n < 2, last, 0)
    copies = []
    for t, src in enumerate((vol, tan)):
        for plane, face in ((odd, s_o), (1 - odd, s_e)):
            for half in range(2):
                rows = pl.ds(2 * half, 2)
                copies.append((src.at[plane, rows], face.at[t, rows]))
        copies += [(src.at[:, row_c], s_c.at[:, t]), (src.at[:, row_m], s_m.at[:, t])]
    run_copies(copies, sems)()


def weights_kernel(vol, tan, sw, dw, t_s, t_d, own, dw_half, sw_all, band, dband, sem, sems):
    n = lax.axis_index("narrow")
    wait = run_copies([(vol, own.at[0]), (tan, own.at[1])], sems)
    shallow = pltpu.make_async_copy(sw, sw_all, sem.at[0])
    deep = pltpu.make_async_copy(
        dw.at[:, :, :, :, pl.ds(pl.multiple_of((n // 2) * 128, 128), 128)], dw_half, sem.at[1]
    )
    shallow.start()
    deep.start()
    band[...] = jnp.zeros_like(band)
    dband[...] = jnp.zeros_like(dband)
    nt = (((1,), (1,)), ((), ()))

    def build(source, scratch, pick, out):
        for a in range(3):
            for c in range(3):
                for b in range(3):
                    scratch[a * 3 + c, 64 * (b + 1) : 64 * (b + 2), :] = source[a, b, c]
                for r in range(2):
                    rows = scratch[a * 3 + c, 64 * (1 - r) : 64 * (1 - r) + 256, :]
                    placed = lax.dot_general(pick, rows, nt, preferred_element_type=F32)
                    out[a, c * 128 + r * 64 : c * 128 + r * 64 + 64, :] = placed.astype(BF16)

    def selector(width, shift):
        row = lax.broadcasted_iota(jnp.int32, (64, width), 0)
        col = lax.broadcasted_iota(jnp.int32, (64, width), 1)
        return jnp.where(col == row + shift, 1.0, 0.0).astype(BF16)

    shallow.wait()
    build(sw_all, band, selector(64, 0), t_s)
    deep.wait()
    build(dw_half, dband, selector(128, 64 * lax.rem(n, 2)), t_d)
    wait()


def shifted_sum(acc, lane, first, final):
    rows = acc.shape[0] // 3
    left = pltpu.roll(acc[0:rows], 1, 1)
    right = pltpu.roll(acc[2 * rows :], acc.shape[1] - 1, 1)
    return acc[rows : 2 * rows] + jnp.where(first(lane), 0.0, left) + jnp.where(final(lane), 0.0, right)


def activate(pre, dot):
    s = 0.5 * jnp.tanh(0.5 * pre) + 0.5
    primal = (pre * s).astype(BF16)
    tangent = (s * (1.0 + pre * (1.0 - s)) * dot).astype(BF16)
    return primal, tangent


def pair_matrix(cells):
    source = lax.broadcasted_iota(jnp.int32, (cells, cells // 2), 0)
    target = lax.broadcasted_iota(jnp.int32, (cells, cells // 2), 1)
    return jnp.where(source // 2 == target, 0.125, 0.0).astype(BF16)


def pool_plane(out, pairing):
    halves = [jnp.dot(value, pairing, preferred_element_type=F32) for value in out]
    return jnp.concatenate(halves, axis=1)


def shallow_lanes(cells):
    lane = lax.broadcasted_iota(jnp.int32, (128, cells), 1)
    return lane, (lambda v: v == 0), (lambda v: v == cells - 1)


def row_windows(face, core_row, far_row, n, narrow):
    rows, chans, cells = face.shape
    far_row = jnp.where((n > 0) & (n < narrow - 1), far_row, jnp.zeros_like(far_row))
    even = lax.rem(n, 2) == 0
    top, bottom = jnp.where(even, far_row, core_row), jnp.where(even, core_row, far_row)
    flat = face.reshape(rows * chans, cells)
    return (
        jnp.concatenate([top, flat[: 3 * chans]], axis=0),
        jnp.concatenate([flat[chans:], bottom], axis=0),
    )


def edge_kernel(face, *rest):
    row_c, row_m = rest[-2:]
    n = lax.axis_index("narrow")
    last = face.shape[1] - 1
    for t in range(2):
        for row, is_last in ((row_c, lax.rem(n, 2) == 0), (row_m, n < 2)):
            chans = face.shape[2]
            row[t, 0:chans] = jnp.where(is_last, face[t, last], face[t, 0])
            if row.shape[1] > chans:
                row[t, chans:] = jnp.zeros((row.shape[1] - chans, face.shape[3]), BF16)


def own_kernel(narrow, x, r_c, r_m, t_s, part):
    n = lax.axis_index("narrow")
    cells = x.shape[4]
    lane, first, final = shallow_lanes(cells)
    for t in range(2):
        stacks = [row_windows(x[t, p], r_c[p, t], r_m[p, t], n, narrow) for p in range(2)]
        for win in range(2):
            stack = jnp.concatenate([stacks[0][win], stacks[1][win]], axis=0)
            for q in range(2):
                taps = jnp.concatenate([t_s[1 - q], t_s[2 - q]], axis=1)
                acc = jnp.dot(taps, stack, preferred_element_type=F32)
                part[q, t, win] = shifted_sum(acc, lane, first, final)


def finish_plane(narrow, q, taps, face, core_row, far_row, part, emit):
    n = lax.axis_index("narrow")
    chans, cells = face.shape[2:]
    lane, first, final = shallow_lanes(cells)
    pairing = pair_matrix(cells)
    stacks = []
    for t in range(2):
        far = jnp.zeros((chans, cells), BF16) if far_row is None else far_row[t, 0:chans]
        stacks.append(row_windows(face[t], core_row[t, 0:chans], far, n, narrow))
    for win in range(2):
        pre = []
        for t in range(2):
            acc = jnp.dot(taps, stacks[t][win], preferred_element_type=F32)
            pre.append(part[q, t, win] + shifted_sum(acc, lane, first, final))
        out = activate(*pre)
        emit(win, pre, [v.reshape(2, 64, cells) for v in out], pool_plane(out, pairing))


def near_kernel(narrow, r_e, c_e, m_e, t_s, part, skip_f, skip_t, pool_part):
    odd = lax.rem(lax.axis_index("wide"), 2)

    def emit(win, pre, out, pool):
        for t, ref in enumerate((skip_f, skip_t)):
            ref[2 * win : 2 * win + 2] = out[t]
        pool_part[win] = pool[0:64] + pool[64:128]

    finish_plane(narrow, 1 - odd, t_s[2 - 2 * odd], r_e, c_e, m_e, part, emit)


def far_taps(wide, t_s):
    w = lax.axis_index("wide")
    taps = t_s[2 * lax.rem(w, 2)]
    return jnp.where((w > 0) & (w < wide - 1), taps, jnp.zeros_like(taps))


def far_kernel(wide, narrow, r_o, c_o, t_s, part, pool_part, skip_f, skip_t, pool_far, edge_pre):
    odd = lax.rem(lax.axis_index("wide"), 2)
    even_n = lax.rem(lax.axis_index("narrow"), 2) == 0

    def emit(win, pre, out, pool):
        for t, ref in enumerate((skip_f, skip_t)):
            ref[2 * win : 2 * win + 2] = out[t]
        none = jnp.zeros_like(pool[0:64])
        if win == 0:
            pool_far[0] = pool_part[0] + jnp.where(even_n, none, pool[0:64]) + pool[64:128]
            for t in range(2):
                edge_pre[t] = pre[t][0:64]
        else:
            pool_far[1] = pool_part[1] + pool[0:64] + jnp.where(even_n, pool[64:128], none)
            for t in range(2):
                edge_pre[t] = jnp.where(even_n, edge_pre[t], pre[t][64:128])

    finish_plane(narrow, odd, far_taps(wide, t_s), r_o, c_o, None, part, emit)


def edge_row_kernel(wide, narrow, m_o, t_s, edge_pre, pool_far, edge_f, edge_t, pooled):
    n = lax.axis_index("narrow")
    chans, cells = edge_pre.shape[1:]
    even_n = lax.rem(n, 2) == 0
    has_m = (n > 0) & (n < narrow - 1)
    lane, first, final = shallow_lanes(cells)
    taps = far_taps(wide, t_s)
    upper = jnp.concatenate([taps[2 * c * chans : (2 * c + 1) * chans] for c in range(3)], axis=0)
    lower = jnp.concatenate([taps[(2 * c + 1) * chans : (2 * c + 2) * chans] for c in range(3)], axis=0)
    taps = jnp.where(even_n, upper, lower)
    pre = []
    for t in range(2):
        row = m_o[t, 0:chans]
        row = jnp.where(has_m, row, jnp.zeros_like(row))
        none = jnp.zeros_like(row)
        stack = [jnp.where(even_n, row, none), none, none, jnp.where(even_n, none, row)]
        acc = jnp.dot(taps, jnp.concatenate(stack, axis=0), preferred_element_type=F32)
        pre.append(edge_pre[t] + shifted_sum(acc, lane[0:chans], first, final))
    out = activate(*pre)
    edge_f[...], edge_t[...] = out
    pool = pool_plane(out, pair_matrix(cells))
    for win in range(2):
        mine = even_n if win == 0 else jnp.logical_not(even_n)
        pooled[win] = (pool_far[win] + jnp.where(mine, pool, jnp.zeros_like(pool))).astype(BF16)


def deep_lanes(cells):
    lane = lax.broadcasted_iota(jnp.int32, (128, 2 * cells), 1)
    first = lambda v: (v == 0) | (v == cells)
    final = lambda v: (v == cells - 1) | (v == 2 * cells - 1)
    return lane, first, final


def gather_rows(x, parts, far, narrow):
    n = lax.axis_index("narrow")
    sib = n + 1 - 2 * lax.rem(n, 2)
    pair = parts[0].shape[0]
    x[0] = jnp.zeros(x.shape[1:], BF16)
    x[narrow * pair + 1] = jnp.zeros(x.shape[1:], BF16)
    for k, source in enumerate(parts):
        member = n if k < 2 else sib
        owner = lax.rem(member + 2 * (k % 2), narrow)
        if far is not None:
            owner = jnp.where(far, lax.rem(member + 2 - 2 * (k % 2), narrow), owner)
        x[pl.ds(owner * pair + 1, pair)] = source[...]


def deep_sum(x, taps, j, lane, first, final):
    stack = x[2 * j : 2 * j + 4].reshape(256, x.shape[2])
    acc = jnp.dot(taps, stack, preferred_element_type=F32)
    return shifted_sum(acc, lane, first, final)


def copy_planes(near_f, near_t, far_f, far_t, edge_f, edge_t, skip_f, skip_t, sems):
    odd = lax.rem(lax.axis_index("wide"), 2)
    even_n = lax.rem(lax.axis_index("narrow"), 2) == 0
    last = far_f.shape[0] - 1
    edge, rest = jnp.where(even_n, 0, last), pl.ds(jnp.where(even_n, 1, 0), last)
    copies = []
    for near, far, row, skip in ((near_f, far_f, edge_f, skip_f), (near_t, far_t, edge_t, skip_t)):
        copies += [
            (near, skip.at[1 - odd]),
            (far.at[rest], skip.at[odd, rest]),
            (row, skip.at[odd, edge]),
        ]
    return run_copies(copies, sems)


def deep_near_kernel(narrow, own, across, own_c, across_c, e, e_across, e_c, e_across_c, t_d, total, x, y):
    odd = lax.rem(lax.axis_index("wide"), 2)
    gather_rows(x, (own, across, own_c, across_c), None, narrow)
    gather_rows(y, (e, e_across, e_c, e_across_c), None, narrow)
    cells = x.shape[2]
    lanes = deep_lanes(cells // 2)
    taps = jnp.concatenate([t_d[1], t_d[2 - 2 * odd]], axis=1)
    for j in range(total.shape[0]):
        stack = [v[2 * j : 2 * j + 4].reshape(256, cells) for v in (x, y)]
        acc = jnp.dot(taps, jnp.concatenate(stack, axis=0), preferred_element_type=F32)
        total[j] = shifted_sum(acc, *lanes)


def deep_far_kernel(wide, narrow, o, o_across, o_c, o_across_c, t_d, part, near_f, near_t,
                    far_f, far_t, edge_f, edge_t, out_f, out_t, skip_f, skip_t, x, staged, sems, skip_sems):
    planes = (near_f, near_t, far_f, far_t, edge_f, edge_t, skip_f, skip_t)
    waits = [copy_planes(*planes, skip_sems)]
    w = lax.axis_index("wide")
    cells = x.shape[2] // 2
    far = (w == wide // 2 - 1) | (w == wide // 2)
    gather_rows(x, (o, o_across, o_c, o_across_c), far, narrow)
    lanes = deep_lanes(cells)
    taps = far_taps(wide, t_d)
    for j in range(part.shape[0]):
        both = part[j] + deep_sum(x, taps, j, *lanes)
        out = activate(both[:, :cells], both[:, cells:])
        rows = pl.ds(2 * j, 2)
        copies = []
        for t, ref in enumerate((out_f, out_t)):
            staged[t, 2 * j : 2 * j + 2] = out[t].reshape(2, 64, cells)
            copies.append((staged.at[t, rows], ref.at[0, rows]))
        waits.append(run_copies(copies, sems.at[j]))
    for wait in waits:
        wait()


def call(body, outs, in_specs, out_specs, scratch=()):
    return pl.pallas_call(
        body,
        out_shape=[o if hasattr(o, "dtype") else jax.ShapeDtypeStruct(o, BF16) for o in outs],
        in_specs=in_specs,
        out_specs=out_specs,
        scratch_shapes=list(scratch),
        compiler_params=pltpu.CompilerParams(vmem_limit_bytes=32 * 1024 * 1024),
        cost_estimate=pl.CostEstimate(flops=0, bytes_accessed=0, transcendentals=0),
    )


def local(wide, narrow, volume, volume_tangent, shallow_weight, deep_weight):
    planes, rows, chans, cells = volume.shape
    volume, volume_tangent, shallow_weight, deep_weight = (
        pltpu.with_memory_space_constraint(v, pltpu.HBM)
        for v in (volume, volume_tangent, shallow_weight, deep_weight)
    )
    dma = pltpu.SemaphoreType.DMA

    def swap(v, kind, route):
        return lax.ppermute(v, BOTH, exchange(wide, narrow, kind, route))

    def full(*shape):
        return jax.ShapeDtypeStruct(shape, F32)

    plane, edge = (rows, chans, cells), (planes, 2, chans, cells)
    s_o, s_e, s_c, s_m = call(
        slices_kernel, [(2,) + plane, (2,) + plane, edge, edge],
        [HBM] * 2, [ANY] * 4, [dma((12,))],
    )(volume, volume_tangent)
    r_o = swap(s_o, "O", "same")
    r_e = swap(s_e, "E", "same")
    r_c = swap(s_c, "", "core")
    r_m = swap(s_m, "", "mirror")
    band = (3, 384, 256)
    t_s, t_d, own = call(
        weights_kernel, [band, band, (2,) + volume.shape], [HBM] * 4, [VMEM, VMEM, ANY],
        [
            pltpu.VMEM((3, 3, 3, 64, 128), BF16),
            pltpu.VMEM((3, 3, 3, 64, 64), BF16),
            pltpu.VMEM((9, 320, 64), BF16),
            pltpu.VMEM((9, 320, 128), BF16),
            dma((2,)),
            dma((2,)),
        ],
    )(volume, volume_tangent, shallow_weight, deep_weight)
    wins = rows // 2
    (part,) = call(
        functools.partial(own_kernel, narrow),
        [full(planes, 2, wins, 128, cells)], [VMEM] * 4, [VMEM],
    )(own, r_c, r_m, t_s)
    row_ec, row_em = call(edge_kernel, [(2, chans + PAD, cells)] * 2, [VMEM], [VMEM] * 2)(r_e)
    c_e, m_e = swap(row_ec, "", "core"), swap(row_em, "", "corner")
    row_oc, row_om = call(edge_kernel, [(2, chans, cells)] * 2, [VMEM] * 3, [VMEM] * 2)(r_o, part, row_ec)
    m_o = swap(row_om, "", "corner")
    c_o = swap(row_oc, "", "core")
    near_f, near_t, pool_part = call(
        functools.partial(near_kernel, narrow),
        [plane, plane, full(wins, chans, cells)], [VMEM] * 5, [VMEM] * 3,
    )(r_e, c_e, m_e, t_s, part)
    far_f, far_t, pool_far, edge_pre = call(
        functools.partial(far_kernel, wide, narrow),
        [plane, plane, full(wins, chans, cells), full(2, chans, cells)], [VMEM] * 5, [VMEM] * 4,
    )(r_o, c_o, t_s, part, pool_part)
    edge_f, edge_t, pooled = call(
        functools.partial(edge_row_kernel, wide, narrow),
        [(chans, cells)] * 2 + [(wins, chans, cells)], [VMEM] * 4, [VMEM] * 3,
    )(m_o, t_s, edge_pre, pool_far)
    o2 = swap(pooled, "O", "near")
    e2 = swap(pooled, "E", "same")
    across = swap(pooled, "", "across")
    e_across = swap(e2, "", "across")
    o_across = swap(o2, "", "across")
    own_c, across_c = swap(pooled, "", "core"), swap(across, "", "core")
    e_c, e_across_c = swap(e2, "", "core"), swap(e_across, "", "core")
    o_c, o_across_c = swap(o2, "", "core"), swap(o_across, "", "core")
    deep_rows = wins * narrow
    sums = full(deep_rows // 2, 128, cells)
    gathered = pltpu.VMEM((deep_rows + 2, chans, cells), BF16)
    (total_d,) = call(
        functools.partial(deep_near_kernel, narrow),
        [sums], [VMEM] * 9, [VMEM], [gathered, gathered],
    )(pooled, across, own_c, across_c, e2, e_across, e_c, e_across_c, t_d)
    deep_shape = (1, deep_rows, 64, cells // 2)
    staged = pltpu.VMEM((2, deep_rows, 64, cells // 2), BF16)
    deep_f, deep_t, skip_f, skip_t = call(
        functools.partial(deep_far_kernel, wide, narrow),
        [deep_shape, deep_shape, volume.shape, volume.shape], [VMEM] * 12, [HBM] * 4,
        [gathered, staged, dma((deep_rows // 2, 2)), dma((6,))],
    )(o2, o_across, o_c, o_across_c, t_d, total_d, near_f, near_t, far_f, far_t, edge_f, edge_t)
    return skip_f, skip_t, deep_f, deep_t


def solution(mesh):
    wide, narrow = mesh.shape["wide"], mesh.shape["narrow"]
    in_specs = (P("wide", "narrow", None, None), P("wide", "narrow", None, None), P(), P())
    out_specs = (
        P("wide", "narrow", None, None),
        P("wide", "narrow", None, None),
        P("wide", None, "narrow", None),
        P("wide", None, "narrow", None),
    )
    return jax.shard_map(
        functools.partial(local, wide, narrow), mesh=mesh, in_specs=in_specs, out_specs=out_specs,
        check_vma=False,
    )
```
